32 devices in a mesh: seq: 4 (over z), fsdp: 8 (over y, x, core).
Axes of the slice: x: 2, y: 2, z: 4, core: 2. Of those that a mesh axis runs over, the one named last changes fastest.
Arguments:
- tokens: bfloat16 [8, 1536, 2048], P('fsdp', 'seq'), may hold values from -6 to 6
- cotangent: bfloat16 [8, 1536, 2048], P('fsdp', 'seq'), may hold values from -6 to 6
- doc_lengths: int32 [8, 3], P('fsdp'), may hold values from 1 to 1534, as said below
- routes: int32 [8, 1536, 8], P('fsdp', 'seq'), may hold values from 0 to 15, all different within a row; in each aligned block of 384 rows (0 to 383, 384 to 767, ..., all dimensions but the last counted through in order) at most 256 rows name the same one
- attn_weight: bfloat16 [2048, 8192], P(('seq', 'fsdp'))
- router_weight: bfloat16 [2048, 16], P(('seq', 'fsdp')), may hold values from -0.0625 to 0.0625
- gain_values: bfloat16 [4352], P(('seq', 'fsdp')), may hold values from 0.5 to 1.5
- expert_weight: bfloat16 [16, 2048, 3072], P('fsdp', 'seq')
- attn_first: float32 [2048, 8192], P(('seq', 'fsdp'))
- attn_second: float32 [2048, 8192], P(('seq', 'fsdp'))
- router_first: float32 [2048, 16], P(('seq', 'fsdp'))
- router_second: float32 [2048, 16], P(('seq', 'fsdp'))
- gain_first: float32 [4352], P(('seq', 'fsdp'))
- gain_second: float32 [4352], P(('seq', 'fsdp'))
- expert_first: float32 [16, 2048, 3072], P('fsdp', 'seq')
- expert_second: float32 [16, 2048, 3072], P('fsdp', 'seq')
Outputs:
- layer_out: bfloat16 [8, 1536, 2048], P('fsdp', 'seq')
- input_grad: float32 [8, 1536, 2048], P('fsdp', 'seq')
- attn_moment: float32 [2048, 8192], P(('seq', 'fsdp'))
- attn_square: float32 [2048, 8192], P(('seq', 'fsdp'))
- attn_master: float32 [2048, 8192], P(('seq', 'fsdp'))
- router_moment: float32 [2048, 16], P(('seq', 'fsdp'))
- router_square: float32 [2048, 16], P(('seq', 'fsdp'))
- router_master: float32 [2048, 16], P(('seq', 'fsdp'))
- gain_moment: float32 [4352], P(('seq', 'fsdp'))
- gain_square: float32 [4352], P(('seq', 'fsdp'))
- gain_master: float32 [4352], P(('seq', 'fsdp'))
- expert_moment: float32 [16, 2048, 3072], P('fsdp', 'seq')
- expert_square: float32 [16, 2048, 3072], P('fsdp', 'seq')
- expert_master: float32 [16, 2048, 3072], P('fsdp', 'seq')
The draws below stay inside these ranges and needn't reach their ends.
Inputs may be any that keep to these rules, and one draw needn't show every extreme that they name: `routes`: each token names 8 different experts; among the 384 tokens of one device (aligned blocks of a sequence) no expert is named more than 256 times, a bound that some block reaches. `doc_lengths`: the three lengths sum to 1536; the first and the last are at most 192; in some sequence both are 1.
All inputs are finite; a program needn't handle non-finite values.
Results may differ from the reference program's by a relative error of at most 0.02.
Values may be sent and summed in bfloat16 or wider, within the bound.
No kernel may reach another device: no remote copies, remote signals or barrier semaphores. Data moves between devices by JAX's collectives and lax.ppermute only.
A program may use at most 512 MiB of HBM per device.

```python
import math
import jax
import jax.numpy as jnp
import numpy as np
from jax import lax

D = 2048
HEADS = 16
HDIM = 128
FFE = 1024
TOP = 8
STEP = 10
LENGTH = 1536
TOK_DEV = 384
SEQS = 8
TOKENS = 12288
EXPERTS = 16
CAP = 256
GAINS = 4352
N_SEQ = 4


RATIO_FIRST = 1.0 / 9.0


RATIO_SECOND = 1.0 / 19.0


SECOND_LOW = 0.5


SECOND_HIGH = 8.0


def normal_field(key, shape):
    return jnp.clip(jax.random.normal(key, shape, jnp.float32), -6.0, 6.0)


def log_factor(key, shape):
    return jnp.exp(jax.random.uniform(key, shape, jnp.float32, math.log(SECOND_LOW), math.log(SECOND_HIGH)))


def attention_scale(inner_scale, outer_scale):
    column = jnp.arange(4 * D)
    return jnp.where(column < 3 * D, inner_scale, outer_scale)[None, :]


def expert_scale(inner_scale, outer_scale):
    column = jnp.arange(3 * FFE)
    return jnp.where(column < 2 * FFE, inner_scale, outer_scale)[None, None, :]


def attention_grad_scale():
    return attention_scale(math.sqrt(TOKENS), math.sqrt(TOKENS) / 16.0)


def expert_grad_scale():
    routed = math.sqrt(TOKENS * TOP / EXPERTS)
    return expert_scale(routed, routed / 10.0)


def router_grad_scale():
    return 27.0 * math.sqrt(TOKENS * TOP / EXPERTS)


def gain_grad_scale():
    return 3.0 * math.sqrt(TOKENS)


def draw_doc_lengths(key, part):
    key = jax.random.fold_in(key, 7)
    key_first, key_last, key_pick = jax.random.split(key, 3)
    first_len = jax.random.randint(key_first, (SEQS, 1), 1, TOK_DEV // 2 + 1)
    last_len = jax.random.randint(key_last, (SEQS, 1), 1, TOK_DEV // 2 + 1)
    chosen_seq = jax.random.randint(key_pick, (), 0, SEQS)
    is_chosen = (jnp.arange(SEQS, dtype=jnp.int32) == chosen_seq)[:, None]
    first_len = jnp.where(is_chosen, 1, first_len)
    last_len = jnp.where(is_chosen, 1, last_len)
    return jnp.concatenate([first_len, LENGTH - first_len - last_len, last_len], axis=1).astype(jnp.int32)


def draw_attn_weight(key, part):
    key = jax.random.fold_in(key, 11)
    shape = (D, 4 * D)
    base = normal_field(key, shape)
    return (base * attention_scale(D ** (-0.5), 16.0 * D ** (-0.5))).astype(jnp.bfloat16)


def draw_expert_weight(key, part):
    key = jax.random.fold_in(key, 13)
    shape = (EXPERTS, D, 3 * FFE)
    base = normal_field(key, shape)
    return (base * expert_scale(D ** (-0.5), 8.0 * FFE ** (-0.5))).astype(jnp.bfloat16)


def draw_attn_first(key, part):
    key = jax.random.fold_in(key, 17)
    shape = (D, 4 * D)
    base = normal_field(key, shape)
    return base * RATIO_FIRST * attention_grad_scale()


def draw_attn_second(key, part):
    key = jax.random.fold_in(key, 19)
    shape = (D, 4 * D)
    factor = log_factor(key, shape)
    scale = attention_grad_scale()
    return factor * RATIO_SECOND * scale * scale


def draw_router_first(key, part):
    key = jax.random.fold_in(key, 23)
    shape = (D, EXPERTS)
    base = normal_field(key, shape)
    return base * RATIO_FIRST * router_grad_scale()


def draw_router_second(key, part):
    key = jax.random.fold_in(key, 29)
    shape = (D, EXPERTS)
    factor = log_factor(key, shape)
    scale = router_grad_scale()
    return factor * RATIO_SECOND * scale * scale


def draw_gain_first(key, part):
    key = jax.random.fold_in(key, 31)
    shape = (GAINS,)
    base = normal_field(key, shape)
    return base * RATIO_FIRST * gain_grad_scale()


def draw_gain_second(key, part):
    key = jax.random.fold_in(key, 37)
    shape = (GAINS,)
    factor = log_factor(key, shape)
    scale = gain_grad_scale()
    return factor * RATIO_SECOND * scale * scale


def draw_expert_first(key, part):
    key = jax.random.fold_in(key, 41)
    shape = (EXPERTS, D, 3 * FFE)
    base = normal_field(key, shape)
    return base * RATIO_FIRST * expert_grad_scale()


def draw_expert_second(key, part):
    key = jax.random.fold_in(key, 43)
    shape = (EXPERTS, D, 3 * FFE)
    factor = log_factor(key, shape)
    scale = expert_grad_scale()
    return factor * RATIO_SECOND * scale * scale


def strengthened(drawn, key, source, target, blocks, factor):
    def block_of(axis_at):
        return (jnp.arange(drawn.shape[axis_at]) // (drawn.shape[axis_at] // blocks)).reshape((-1,) + (1,) * (drawn.ndim - 1 - axis_at))

    near = jax.random.permutation(key, blocks)[block_of(target)]
    other_side = (block_of(target) + blocks // 2) % blocks
    return jnp.where((block_of(source) == near) | (block_of(source) == other_side), factor * drawn, drawn)


def block_levels(stream_key, shape, cuts, smallest, largest):
    loudness, own = 1.0, jax.random.fold_in(stream_key, 6)
    for axis_at, shards_of in cuts:
        steps = jnp.exp(jax.random.uniform(jax.random.fold_in(own, axis_at), (shards_of,), jnp.float32, smallest / len(cuts), largest / len(cuts)))
        loudness = loudness * jnp.repeat(steps, shape[axis_at] // shards_of).reshape([-1 if axis == axis_at else 1 for axis in range(len(shape))])
    return loudness


def routed_block(rng, own, number, rows, number_of, top, most, skew):
    ranking = jax.random.permutation(rng, number_of)
    crowded, ordinary = portions_of(number_of, rows * top, most, skew, True), portions_of(number_of, rows * top, most, skew, False)
    places = jnp.arange(number_of)

    def named(sizes, offset_by):
        used = int((sizes > 0).sum())
        fixed = max(1, used // 4)
        passed = fixed + (places - fixed + offset_by * (used - fixed)) % max(1, number_of - fixed)
        return jnp.zeros((number_of,), jnp.int32).at[ranking[jnp.where(places < fixed, places, passed)]].set(jnp.asarray(sizes, jnp.int32))

    sizes = jnp.where(number % 4 == 0, named(crowded, number // 4), named(ordinary, number - number // 4 - 1))
    mixed = jax.random.permutation(jax.random.fold_in(own, 3), number_of)
    giver, sink = mixed[0:number_of // 2 * 2:2], mixed[1:number_of // 2 * 2:2]
    room = jnp.minimum(sizes[giver] - 1, most - sizes[sink]) // 2
    room = jnp.where((giver == ranking[0]) | (sink == ranking[0]) | (sizes[sink] == 0), 0, jnp.maximum(room, 0))
    passed = jax.random.randint(jax.random.fold_in(own, 4), (number_of // 2,), 0, 1 << 20) % (room + 1)
    sizes = sizes.at[giver].add(-passed).at[sink].add(passed)
    labels = jnp.searchsorted(jnp.cumsum(sizes), jnp.arange(rows * top), side="right").astype(jnp.int32)
    listing = labels.reshape(top, rows).T
    listing = listing[jax.random.permutation(jax.random.fold_in(own, 1), rows)]
    offset_by = jax.random.randint(jax.random.fold_in(own, 2), (rows, 1), 0, top)
    return jnp.take_along_axis(listing, (jnp.arange(top)[None, :] + offset_by) % top, axis=1)


def portions_of(number_of, total, limit, slope, full):
    loads = [(1 << 20) // math.isqrt(rank ** slope) + 1 for rank in range(1, number_of + 1)]
    largest = limit if full else min(limit, max(-(-total // number_of), total * loads[0] // sum(loads)))
    least = 1 if total - largest >= number_of - 1 else 0
    counts, surplus = [largest] + [least] * (number_of - 1), total - largest - least * (number_of - 1)
    while surplus > 0:
        movable = [i for i in range(1, number_of) if counts[i] < largest] or [i for i in range(1, number_of) if counts[i] < limit]
        pool, remaining = sum([loads[i] for i in movable]), surplus
        for i in movable:
            addition = min(limit - counts[i], max(1, remaining * loads[i] // pool), surplus)
            counts[i] = counts[i] + addition
            surplus = surplus - addition
    return np.array(counts)


def gaussian(key, dims, spread, most, cuts=(), kind=jnp.bfloat16):
    values = jax.random.normal(key, dims, jnp.float32) * spread
    if len(cuts) > 0:
        values = block_levels(key, dims, cuts, -0.22, 0.18) * values
    return jnp.clip(values, min=-most, max=most).astype(kind)


def gaussian_with(key, dims, scale, most, cuts, heavy, kind=jnp.bfloat16):
    drawn = scale * jax.random.normal(key, dims, jnp.float32)
    if cuts:
        drawn = drawn * block_levels(key, dims, cuts, -0.22, 0.18)
    return jnp.clip(strengthened(drawn, jax.random.fold_in(key, 3), *heavy), -most, most).astype(kind)


def setup_inputs(seed: int = 0) -> dict:
    arg_keys = jax.random.split(jax.random.key(seed), 17)
    tokens = gaussian_with(arg_keys[0], (SEQS, LENGTH, D), 1.0, 6.0, ((0, 8), (1, 4)), (0, 2, 8, 2.0))
    cotangent = gaussian(arg_keys[1], (SEQS, LENGTH, D), 1.0, 6.0, ((0, 8), (1, 4)))
    doc_lengths = draw_doc_lengths(jax.random.fold_in(arg_keys[16], 71), 0)
    routes_keys = jax.random.split(jax.random.fold_in(arg_keys[3], 1), SEQS * LENGTH // TOK_DEV)
    routes_turns = jax.random.permutation(jax.random.fold_in(arg_keys[3], 3), SEQS * LENGTH // TOK_DEV)
    routes = jax.vmap(lambda own, number: routed_block(jax.random.fold_in(arg_keys[3], 2), own, number, TOK_DEV, EXPERTS, TOP, CAP, 1))(routes_keys, routes_turns).reshape((SEQS, LENGTH, TOP))
    attn_weight = draw_attn_weight(jax.random.fold_in(arg_keys[16], 71), 0)
    router_weight = gaussian(arg_keys[5], (D, EXPERTS), (4 * D) ** -0.5, 0.0625, ((0, 32),))
    gain_values = jnp.clip(1.0 + 0.1 * jax.random.normal(arg_keys[6], (GAINS,), jnp.float32), 0.5, 1.5).astype(jnp.bfloat16)
    expert_weight = draw_expert_weight(jax.random.fold_in(arg_keys[16], 71), 0)
    attn_first = draw_attn_first(jax.random.fold_in(arg_keys[16], 71), 0)
    attn_second = draw_attn_second(jax.random.fold_in(arg_keys[16], 71), 0)
    router_first = draw_router_first(jax.random.fold_in(arg_keys[16], 71), 0)
    router_second = draw_router_second(jax.random.fold_in(arg_keys[16], 71), 0)
    gain_first = draw_gain_first(jax.random.fold_in(arg_keys[16], 71), 0)
    gain_second = draw_gain_second(jax.random.fold_in(arg_keys[16], 71), 0)
    expert_first = draw_expert_first(jax.random.fold_in(arg_keys[16], 71), 0)
    expert_second = draw_expert_second(jax.random.fold_in(arg_keys[16], 71), 0)
    return dict(tokens=tokens, cotangent=cotangent, doc_lengths=doc_lengths, routes=routes, attn_weight=attn_weight, router_weight=router_weight, gain_values=gain_values, expert_weight=expert_weight, attn_first=attn_first, attn_second=attn_second, router_first=router_first, router_second=router_second, gain_first=gain_first, gain_second=gain_second, expert_first=expert_first, expert_second=expert_second)


NORM_EPS = 1e-06
ROPE_BASE = 10000.0
BETA_ONE = 0.9
BETA_TWO = 0.95
ADAM_EPS = 1e-08
WEIGHT_DECAY = 0.1
RATE_ATTN = 0.1
RATE_ROUTER = 0.03
RATE_GAIN = 0.5
RATE_EXPERT = 0.1
PRECISE = lax.Precision.HIGHEST

@jax.custom_vjp
def low(v):
    return lax.optimization_barrier(v.astype(jnp.bfloat16)).astype(jnp.float32)

@jax.custom_vjp
def low_back(v):
    return v

def low_keep(v):
    return (low(v), None)

def low_pass(kept, grad):
    return (grad,)

def back_keep(v):
    return (v, None)

def back_low(kept, grad):
    return (low(grad),)
low.defvjp(low_keep, low_pass)
low_back.defvjp(back_keep, back_low)

def norm_rows(values, gain_vector):
    return values * lax.rsqrt(lax.optimization_barrier(jnp.mean(values * values, axis=-1, keepdims=True)) + NORM_EPS) * gain_vector

def rotate(values, positions):
    half_width = values.shape[-1] // 2
    frequency = ROPE_BASE ** (-jnp.arange(half_width, dtype=jnp.float32) / half_width)
    angles = positions[:, None] * frequency[None, :]
    cosine = jnp.cos(angles)[:, None, :]
    sine_part = jnp.sin(angles)[:, None, :]
    first_half = values[..., :half_width]
    second_half = values[..., half_width:]
    return jnp.concatenate([first_half * cosine - second_half * sine_part, first_half * sine_part + second_half * cosine], axis=-1)

def slot_tables(row_routes):
    pair_routes = row_routes.reshape(N_SEQ, TOK_DEV * TOP)
    pair_hot = (pair_routes[:, :, None] == jnp.arange(EXPERTS, dtype=jnp.int32)[None, None, :]).astype(jnp.int32)
    before = jnp.cumsum(pair_hot, axis=1) - pair_hot
    slot_index = lax.optimization_barrier(jnp.sum(before * pair_hot, axis=2))
    blocks = jnp.arange(N_SEQ, dtype=jnp.int32)[:, None]
    target = (pair_routes * (N_SEQ * CAP) + blocks * CAP + slot_index).reshape(LENGTH * TOP).astype(jnp.int32)
    owners = (jnp.arange(LENGTH * TOP, dtype=jnp.int32) // TOP).astype(jnp.int32)
    source = jnp.full((EXPERTS * N_SEQ * CAP,), LENGTH, dtype=jnp.int32).at[target].set(owners)
    return (target, source)

def sequence_forward(weight_set, row_tokens, row_routes, row_target, row_source, row_doc):
    attn_all, router_all, gain_all, expert_all = weight_set
    attn_gain = gain_all[:D]
    ffn_gain = gain_all[D:2 * D]
    query_gain = gain_all[2 * D:2 * D + HDIM]
    key_gain = gain_all[2 * D + HDIM:]
    token_place = jnp.arange(LENGTH, dtype=jnp.int32)
    positions = token_place.astype(jnp.float32)
    doc_index = (token_place >= row_doc[0]).astype(jnp.int32) + (token_place >= row_doc[0] + row_doc[1]).astype(jnp.int32)
    same_doc = doc_index[:, None] == doc_index[None, :]
    normed_one = low(norm_rows(row_tokens, attn_gain))
    project = low_back(jnp.dot(normed_one, attn_all[:, :3 * D], precision=PRECISE))
    query_pre = project[:, :D].reshape(LENGTH, HEADS, HDIM)
    key_pre = project[:, D:2 * D].reshape(LENGTH, HEADS, HDIM)
    value_pre = project[:, 2 * D:].reshape(LENGTH, HEADS, HDIM)
    query_rot = low(low_back(rotate(norm_rows(query_pre, query_gain), positions)))
    key_rot = low(low_back(rotate(norm_rows(key_pre, key_gain), positions)))
    value_rot = low(low_back(value_pre))
    raw_scores = low_back(jnp.einsum('ihd,jhd->hij', query_rot, key_rot, precision=PRECISE) * HDIM ** (-0.5))
    masked = jnp.where(same_doc[None, :, :], raw_scores, -1e+30)
    row_top = lax.optimization_barrier(jnp.max(masked, axis=2, keepdims=True))
    exponent = jnp.exp(masked - row_top)
    attend_weights = low(exponent / lax.optimization_barrier(jnp.sum(exponent, axis=2, keepdims=True)))
    attended = jnp.einsum('hij,jhd->ihd', attend_weights, value_rot, precision=PRECISE).reshape(LENGTH, D)
    attended = low(low_back(attended))
    branch = low_back(jnp.dot(attended, attn_all[:, 3 * D:], precision=PRECISE))
    middle = row_tokens + branch
    normed_two = low(norm_rows(middle, ffn_gain))
    logits = low_back(jnp.dot(normed_two, router_all, precision=PRECISE))
    chosen = (row_routes[:, :, None] == jnp.arange(EXPERTS, dtype=jnp.int32)[None, None, :]).astype(jnp.float32)
    picked = lax.optimization_barrier(jnp.sum(chosen * logits[:, None, :], axis=2))
    gate_weights = jax.nn.softmax(picked, axis=1)
    padded = jnp.concatenate([normed_two, jnp.zeros((1, D), jnp.float32)], axis=0)
    expert_rows = low_back(padded[row_source].reshape(EXPERTS, N_SEQ * CAP, D))
    gate_up = low_back(jnp.einsum('erd,edf->erf', expert_rows, expert_all[:, :, :2 * FFE], precision=PRECISE))
    hidden_mid = low(jax.nn.silu(gate_up[:, :, :FFE]) * gate_up[:, :, FFE:])
    produced = low(low_back(jnp.einsum('erf,edf->erd', hidden_mid, expert_all[:, :, 2 * FFE:], precision=PRECISE)))
    picked_rows = produced.reshape(EXPERTS * N_SEQ * CAP, D)[row_target].reshape(LENGTH, TOP, D)
    mixture = lax.optimization_barrier(jnp.sum(gate_weights[:, :, None] * picked_rows, axis=1))
    return middle + mixture

def adam_step(weight, gradient, first_state, second, step_rate):
    first_new = BETA_ONE * first_state + (1.0 - BETA_ONE) * gradient
    second_new = BETA_TWO * second + (1.0 - BETA_TWO) * gradient * gradient
    first_hat = first_new / (1.0 - BETA_ONE ** STEP)
    second_hat = second_new / (1.0 - BETA_TWO ** STEP)
    master = weight.astype(jnp.float32) * (1.0 - step_rate * WEIGHT_DECAY) - step_rate * first_hat / (jnp.sqrt(second_hat) + ADAM_EPS)
    return (first_new, second_new, master)

def reference(tokens, cotangent, doc_lengths, routes, attn_weight, router_weight, gain_values, expert_weight, attn_first, attn_second, router_first, router_second, gain_first, gain_second, expert_first, expert_second):
    weights = (attn_weight.astype(jnp.float32), router_weight.astype(jnp.float32), gain_values.astype(jnp.float32), expert_weight.astype(jnp.float32))
    targets, sources = jax.vmap(slot_tables)(routes)

    def whole(weight_set, token_set):

        def one_sequence(pieces):
            row_tokens, row_routes, row_target, row_source, row_doc = pieces
            return sequence_forward(weight_set, row_tokens, row_routes, row_target, row_source, row_doc)
        return lax.map(jax.checkpoint(one_sequence), (token_set, routes, targets, sources, doc_lengths))
    result, pull = jax.vjp(whole, weights, tokens.astype(jnp.float32))
    weight_grads, input_grad = pull(cotangent.astype(jnp.float32))
    attn_grad, router_grad, gain_grad, expert_grad = weight_grads
    attn_moment, attn_square, attn_master = adam_step(attn_weight, attn_grad, attn_first, attn_second, RATE_ATTN)
    router_moment, router_square, router_master = adam_step(router_weight, router_grad, router_first, router_second, RATE_ROUTER)
    gain_moment, gain_square, gain_master = adam_step(gain_values, gain_grad, gain_first, gain_second, RATE_GAIN)
    expert_moment, expert_square, expert_master = adam_step(expert_weight, expert_grad, expert_first, expert_second, RATE_EXPERT)
    return (result.astype(jnp.bfloat16), input_grad, attn_moment, attn_square, attn_master, router_moment, router_square, router_master, gain_moment, gain_square, gain_master, expert_moment, expert_square, expert_master)
```

```python
import functools
import math

import jax
import jax.numpy as jnp
from jax import lax
from jax.experimental import pallas as pl
from jax.experimental.pallas import tpu as pltpu
from jax.sharding import PartitionSpec as P

HEADS = 16
HDIM = 128
FFE = 1024
TOP = 8
EXP_DEV = 2
STEP = 10

NORM_EPS = 1e-06
ROPE_BASE = 10000.0
BETA_ONE = 0.9
BETA_TWO = 0.95
ADAM_EPS = 1e-08
WEIGHT_DECAY = 0.1
RATE_ATTN = 0.1
RATE_ROUTER = 0.03
RATE_GAIN = 0.5
RATE_EXPERT = 0.1
VMEM_LIMIT = 56 * 1024 * 1024

BRIEF = pl.CostEstimate(flops=1000, bytes_accessed=1000, transcendentals=0)

F32 = jnp.float32
BF16 = jnp.bfloat16


def dot(a, b, ca, cb):
    return lax.dot_general(a, b, (((ca,), (cb,)), ((), ())), preferred_element_type=F32)


def adam_step(weight, gradient, first_state, second, step_rate):
    gradient = gradient.astype(F32)
    first_new = BETA_ONE * first_state + (1.0 - BETA_ONE) * gradient
    second_new = BETA_TWO * second + (1.0 - BETA_TWO) * gradient * gradient
    first_hat = first_new / (1.0 - BETA_ONE**STEP)
    second_hat = second_new / (1.0 - BETA_TWO**STEP)
    master = weight.astype(F32) * (1.0 - step_rate * WEIGHT_DECAY) - step_rate * first_hat / (
        jnp.sqrt(second_hat) + ADAM_EPS
    )
    return first_new, second_new, master


def swap(value, step, axis, count):
    return lax.ppermute(value, axis, [(i, i ^ step) for i in range(count)])


def gather_direct(value, axis, count):
    return jnp.stack([value] + [swap(value, k, axis, count) for k in range(1, count)])


def exchange(parts, axis, count):
    return [parts[0]] + [swap(parts[k], k, axis, count) for k in range(1, count)]


def reorder(stacked, index, axis=0):
    return jnp.take(stacked, index, axis=axis, mode="clip")


def plane_gather(count, value):
    if count != 8:
        whole = lax.all_gather(value, "fsdp")
        mine = lax.axis_index("fsdp")
        return [lax.dynamic_index_in_dim(whole, mine ^ k, 0, False) for k in range(count)]
    go = functools.partial(swap, axis="fsdp", count=count)
    half = value.shape[0] // 2
    by_x, by_y = go(value, 2), go(value, 4)
    far = jnp.concatenate([go(by_x[:half], 4), go(by_y[half:], 2)], axis=0)
    return [value, go(value, 1), by_x, go(by_x, 1), by_y, go(by_y, 1), far, go(far, 1)]


def scatter_first(count, value):
    return swap(value[1], 1, "fsdp", count) if count == 8 else None


def scatter_rest(count, value, got):
    if count != 8:
        mine = lax.axis_index("fsdp")
        stacked = value.transpose(1, 0, 2, 3).reshape(count, *value.shape[2:])
        stacked = reorder(stacked, mine ^ jnp.arange(count))
        return lax.psum_scatter(stacked, "fsdp", scatter_dimension=0).astype(F32)
    go = functools.partial(swap, axis="fsdp", count=count)
    total = value[0].astype(F32) + got.astype(F32)
    half = total.shape[1] // 2
    top, low = total[:, :half], total[:, half:]
    by_x = go(jnp.stack([top[3], top[1]]).astype(BF16), 2).astype(F32)
    by_y = go(jnp.stack([low[3], low[2]]).astype(BF16), 4).astype(F32)
    y_last = go((top[2] + by_x[0]).astype(BF16), 4).astype(F32)
    x_last = go((low[1] + by_y[0]).astype(BF16), 2).astype(F32)
    return jnp.concatenate([top[0] + by_x[1] + y_last, low[0] + by_y[1] + x_last], axis=0)


def plane_scatter(count, value):
    return scatter_rest(count, value, scatter_first(count, value))


def small_sum(value, shares, planes, seq_count, fsdp_count):
    step = 1
    while step < fsdp_count:
        value = value + swap(value, step, "fsdp", fsdp_count)
        step *= 2
    return sum(exchange([shares(value, planes[m]) for m in range(seq_count)], "seq", seq_count))


def to_plane(value, seq_count, fsdp_count):
    rows, width = value.shape
    members, chunk = fsdp_count // seq_count, rows // fsdp_count
    value = value.reshape(fsdp_count, chunk, width)
    value = lax.all_to_all(value, "fsdp", split_axis=0, concat_axis=0, tiled=True)
    value = value.reshape(seq_count, members * chunk, width)
    value = lax.all_to_all(value, "seq", split_axis=0, concat_axis=0, tiled=True)
    value = value.reshape(seq_count, members, chunk, width).transpose(1, 0, 2, 3)
    return value.reshape(rows, width)


def from_plane(value, here, plane, seq_count, fsdp_count):
    rows, width = value.shape
    members, chunk = fsdp_count // seq_count, rows // fsdp_count
    around, planes = here ^ jnp.arange(fsdp_count), plane ^ jnp.arange(seq_count)
    value = value.reshape(members, seq_count, chunk, width).transpose(1, 0, 2, 3)
    value = reorder(value.reshape(seq_count, members * chunk, width), planes)
    value = jnp.stack(exchange(list(value), "seq", seq_count))
    value = value.reshape(seq_count, members, chunk, width)
    value = reorder(value, planes).reshape(fsdp_count, chunk, width)
    value = jnp.stack(exchange(list(reorder(value, around)), "fsdp", fsdp_count))
    return reorder(value, around).reshape(rows, width)


def from_plane_whole(value, seq_count, fsdp_count):
    rows, width = value.shape
    members, chunk = fsdp_count // seq_count, rows // fsdp_count
    value = value.reshape(members, seq_count, chunk, width).transpose(1, 0, 2, 3)
    value = value.reshape(seq_count, members * chunk, width)
    value = lax.all_to_all(value, "seq", split_axis=0, concat_axis=0, tiled=True)
    value = value.reshape(fsdp_count, chunk, width)
    value = lax.all_to_all(value, "fsdp", split_axis=0, concat_axis=0, tiled=True)
    return value.reshape(rows, width)


def head_norm(value):
    return lax.rsqrt(jnp.mean(value * value, axis=-1, keepdims=True) + NORM_EPS)


def turn(value, cosine, sine):
    return value * cosine + pltpu.roll(value, HDIM // 2, 1) * sine


def project_kernel(
    heads, x_ref, gain_ref, w_ref, cos_ref, sin_ref, gq_ref, gk_ref, a_ref, q_ref, k_ref, v_ref, qp_ref, kp_ref
):
    x = x_ref[...].astype(F32)
    a = (x * head_norm(x) * gain_ref[...]).astype(BF16)
    a_ref[...] = a
    width = heads * HDIM
    cosine, sine = cos_ref[...], sin_ref[...]
    for n, (low_ref, pre_ref, g_ref) in enumerate(((q_ref, qp_ref, gq_ref), (k_ref, kp_ref, gk_ref))):
        part = dot(a, w_ref[:, n * width : (n + 1) * width], 1, 0)
        pre_ref[...] = part
        for h in range(heads):
            cols = slice(h * HDIM, (h + 1) * HDIM)
            one = part[:, cols]
            low_ref[:, cols] = turn(one * head_norm(one) * g_ref[...], cosine, sine).astype(BF16)
    v_ref[...] = dot(a, w_ref[:, 2 * width :], 1, 0).astype(BF16)


def project(x, gain, w, cosine, sine, gain_q, gain_k, block):
    rows, model = x.shape
    width = w.shape[1] // 3
    heads = width // HDIM

    def row(cols):
        return pl.BlockSpec((block, cols), lambda i: (i, 0))

    def whole(shape):
        return pl.BlockSpec(shape, lambda i: (0, 0))

    shape = jax.ShapeDtypeStruct
    return pl.pallas_call(
        functools.partial(project_kernel, heads),
        grid=(rows // block,),
        in_specs=[
            row(model),
            whole((1, model)),
            whole(w.shape),
            row(HDIM),
            row(HDIM),
            whole((1, HDIM)),
            whole((1, HDIM)),
        ],
        out_specs=[row(model), row(width), row(width), row(width), row(width), row(width)],
        out_shape=[
            shape((rows, model), BF16),
            shape((rows, width), BF16),
            shape((rows, width), BF16),
            shape((rows, width), BF16),
            shape((rows, width), F32),
            shape((rows, width), F32),
        ],
        compiler_params=pltpu.CompilerParams(vmem_limit_bytes=VMEM_LIMIT),
        cost_estimate=BRIEF,
        name="project",
    )(x, gain, w, cosine, sine, gain_q, gain_k)


SCORE = HDIM**-0.5


def probabilities(q, k, row_doc, col_doc):
    scores = dot(q, k, 1, 1) * (SCORE * math.log2(math.e))
    weight = jnp.where(row_doc == col_doc, jnp.exp2(scores), 0.0)
    return weight * (1.0 / jnp.sum(weight, axis=1, keepdims=True))


def attend_kernel(block, q_ref, k_ref, v_ref, rd_ref, cd_ref, o_ref):
    k, v = k_ref[0], v_ref[0]

    def step(i, _):
        rows = pl.ds(i * block, block)
        p = probabilities(q_ref[0, rows, :], k, rd_ref[0, rows, :], cd_ref[0])
        o_ref[0, rows, :] = dot(p.astype(BF16), v, 1, 0).astype(BF16)
        return 0

    lax.fori_loop(0, q_ref.shape[1] // block, step, 0)


def attend_back_kernel(block, q_ref, k_ref, v_ref, do_ref, rd_ref, cd_ref, dq_ref, dk_ref, dv_ref, sk_ref, sv_ref):
    k, v = k_ref[0], v_ref[0]
    sk_ref[...] = jnp.zeros_like(sk_ref)
    sv_ref[...] = jnp.zeros_like(sv_ref)

    def step(i, _):
        rows = pl.ds(i * block, block)
        q, do = q_ref[0, rows, :], do_ref[0, rows, :]
        p = probabilities(q, k, rd_ref[0, rows, :], cd_ref[0])
        dp = dot(do, v, 1, 1)
        ds = (p * (dp - jnp.sum(p * dp, axis=1, keepdims=True))).astype(BF16)
        dq_ref[0, rows, :] = (dot(ds, k, 1, 0) * SCORE).astype(BF16)
        sk_ref[...] += dot(ds, q, 0, 0)
        sv_ref[...] += dot(p.astype(BF16), do, 0, 0)
        return 0

    lax.fori_loop(0, q_ref.shape[1] // block, step, 0)
    dk_ref[0] = (sk_ref[...] * SCORE).astype(BF16)
    dv_ref[0] = sv_ref[...].astype(BF16)


def attention_specs(length, width):
    head = pl.BlockSpec((1, length, HDIM), lambda s, h: (s, 0, h))
    row_doc = pl.BlockSpec((1, length, 1), lambda s, h: (s, 0, 0))
    col_doc = pl.BlockSpec((1, 1, length), lambda s, h: (s, 0, 0))
    return head, row_doc, col_doc


def attend(q, k, v, row_doc, col_doc):
    seqs, length, width = q.shape
    head, rd, cd = attention_specs(length, width)
    pairs = seqs * (width // HDIM) * length * length
    return pl.pallas_call(
        functools.partial(attend_kernel, 256),
        grid=(seqs, width // HDIM),
        in_specs=[head, head, head, rd, cd],
        out_specs=head,
        out_shape=jax.ShapeDtypeStruct(q.shape, BF16),
        compiler_params=pltpu.CompilerParams(vmem_limit_bytes=VMEM_LIMIT),
        cost_estimate=BRIEF,
        name="attend",
    )(q, k, v, row_doc, col_doc)


def attend_back(q, k, v, do, row_doc, col_doc):
    seqs, length, width = q.shape
    head, rd, cd = attention_specs(length, width)
    pairs = seqs * (width // HDIM) * length * length
    out = jax.ShapeDtypeStruct(q.shape, BF16)
    return pl.pallas_call(
        functools.partial(attend_back_kernel, 256),
        grid=(seqs, width // HDIM),
        in_specs=[head, head, head, head, rd, cd],
        out_specs=[head, head, head],
        out_shape=[out, out, out],
        scratch_shapes=[pltpu.VMEM((length, HDIM), F32), pltpu.VMEM((length, HDIM), F32)],
        compiler_params=pltpu.CompilerParams(vmem_limit_bytes=VMEM_LIMIT),
        cost_estimate=BRIEF,
        name="attend_back",
    )(q, k, v, do, row_doc, col_doc)


def project_back_kernel(
    heads, dq_ref, dk_ref, dv_ref, qp_ref, kp_ref, cos_ref, sin_ref, gq_ref, gk_ref, w_ref, dp_ref, da_ref, dg_ref
):
    cosine, sine = cos_ref[...], -sin_ref[...]
    width = heads * HDIM

    @pl.when(pl.program_id(0) == 0)
    def _():
        dg_ref[...] = jnp.zeros_like(dg_ref)

    for n, (d_ref, pre_ref, g_ref) in enumerate(((dq_ref, qp_ref, gq_ref), (dk_ref, kp_ref, gk_ref))):
        gain = g_ref[...]
        total = jnp.zeros((1, HDIM), F32)
        for h in range(heads):
            cols = slice(h * HDIM, (h + 1) * HDIM)
            dn = turn(d_ref[:, cols].astype(F32), cosine, sine)
            pre = pre_ref[:, cols]
            scale = head_norm(pre)
            hat = pre * scale
            total += jnp.sum(dn * hat, axis=0, keepdims=True)
            inner = dn * gain
            back = scale * (inner - hat * jnp.mean(inner * hat, axis=1, keepdims=True))
            dp_ref[:, n * width + h * HDIM : n * width + (h + 1) * HDIM] = back.astype(BF16)
        dg_ref[n : n + 1, :] += total
    dp_ref[:, 2 * width :] = dv_ref[...]
    split_chunks(da_ref, slice(None), dot(dp_ref[...], w_ref[...], 1, 1))


def project_back(dq, dk, dv, q_pre, k_pre, cosine, sine, gain_q, gain_k, w, block):
    rows, width = dq.shape
    model = w.shape[0]
    form, result = chunk_form(rows // block, block, model)
    heads = width // HDIM

    def row(cols):
        return pl.BlockSpec((block, cols), lambda i: (i, 0))

    def whole(shape):
        return pl.BlockSpec(shape, lambda i: (0, 0))

    shape = jax.ShapeDtypeStruct
    return pl.pallas_call(
        functools.partial(project_back_kernel, heads),
        grid=(rows // block,),
        in_specs=[row(width)] * 5
        + [row(HDIM), row(HDIM), whole((1, HDIM)), whole((1, HDIM)), whole(w.shape)],
        out_specs=[row(3 * width), form, whole((8, HDIM))],
        out_shape=[shape((rows, 3 * width), BF16), result, shape((8, HDIM), F32)],
        compiler_params=pltpu.CompilerParams(vmem_limit_bytes=VMEM_LIMIT),
        cost_estimate=BRIEF,
        name="project_back",
    )(dq, dk, dv, q_pre, k_pre, cosine, sine, gain_q, gain_k, w)


def join_chunks(ref, cols):
    if len(ref.shape) == 2:
        return ref[:, cols]
    two, half, _, chunk, _ = ref.shape
    return jnp.concatenate([ref[k % 2, k // 2, 0, :, cols] for k in range(two * half)], axis=0)


def split_chunks(ref, cols, value):
    if len(ref.shape) == 2:
        ref[:, cols] = value.astype(BF16)
        return
    two, half, _, chunk, _ = ref.shape
    for k in range(two * half):
        ref[k % 2, k // 2, 0, :, cols] = value[k * chunk : (k + 1) * chunk].astype(BF16)


def chunk_form(blocks, rows, model):
    chunk = rows // blocks
    if chunk % 16:
        return pl.BlockSpec((rows, model), lambda i: (i, 0)), jax.ShapeDtypeStruct((blocks * rows, model), BF16)
    shape = (2, blocks // 2, blocks, chunk, model)
    spec = pl.BlockSpec((2, blocks // 2, 1, chunk, model), lambda i: (0, 0, i, 0, 0))
    return spec, jax.ShapeDtypeStruct(shape, BF16)


def by_owner(value, blocks):
    if value.ndim == 2:
        rows, model = value.shape[0] // blocks, value.shape[1]
        value = value.reshape(blocks, blocks // 2, 2, rows // blocks, model).transpose(2, 1, 0, 3, 4)
    return value.reshape(2, blocks // 2, -1, value.shape[-1])


def expert_kernel(wide, narrow, more, rank_ref, rank_col_ref, gate_ref, x_ref, dz_ref, w_ref, *refs):
    if more:
        old_out_ref, old_dx_ref, *refs = refs
    xg_ref, dy_ref, hm_ref, dgu_ref, out_ref, dx_ref, dgate_ref, dzg_ref, yg_ref, dxe_ref, sum_ref = refs
    rows, model = x_ref.shape
    capacity, feed = hm_ref.shape
    hit = rank_ref[0] == lax.broadcasted_iota(jnp.int32, (capacity, rows), 0)
    sel = hit.astype(F32).astype(BF16)
    sel_back = (rank_col_ref[0] == lax.broadcasted_iota(jnp.int32, (rows, capacity), 1)).astype(F32).astype(BF16)
    gate = jnp.sum(jnp.where(hit, gate_ref[0], 0.0), axis=1, keepdims=True)

    def dispatch(i, _):
        cols = pl.ds(pl.multiple_of(i * wide, wide), wide)
        xg_ref[:, cols] = dot(sel, x_ref[:, cols], 1, 0).astype(BF16)
        dz = dot(sel, dz_ref[:, cols], 1, 0)
        dzg_ref[:, cols] = dz.astype(BF16)
        dy_ref[:, cols] = (gate * dz).astype(BF16)
        return 0

    lax.fori_loop(0, model // wide, dispatch, 0)

    def inner(i, _):
        cols = pl.ds(pl.multiple_of(i * narrow, narrow), narrow)
        ups = pl.ds(pl.multiple_of(feed + i * narrow, narrow), narrow)
        downs = pl.ds(pl.multiple_of(2 * feed + i * narrow, narrow), narrow)
        g = dot(xg_ref[...], w_ref[:, cols], 1, 0)
        u = dot(xg_ref[...], w_ref[:, ups], 1, 0)
        dh = dot(dy_ref[...], w_ref[:, downs], 1, 0)
        sig = 1.0 / (1.0 + jnp.exp(-g))
        silu = g * sig
        hm_ref[:, cols] = (silu * u).astype(BF16)
        dgu_ref[:, cols] = (dh * u * (sig + silu * (1.0 - sig))).astype(BF16)
        dgu_ref[:, ups] = (dh * silu).astype(BF16)
        return 0

    lax.fori_loop(0, feed // narrow, inner, 0)
    sum_ref[...] = jnp.zeros_like(sum_ref)

    def outer(i, _):
        cols = pl.ds(pl.multiple_of(i * narrow, narrow), narrow)
        y = dot(hm_ref[...], w_ref[cols, 2 * feed :], 1, 1).astype(BF16).astype(F32)
        part = y * dzg_ref[:, cols].astype(F32)
        total = part[:, :128]
        for j in range(1, narrow // 128):
            total += part[:, j * 128 : (j + 1) * 128]
        sum_ref[...] += total
        yg_ref[:, cols] = (gate * y).astype(BF16)
        dxe_ref[:, cols] = dot(dgu_ref[...], w_ref[cols, : 2 * feed], 1, 1).astype(BF16)
        return 0

    lax.fori_loop(0, model // narrow, outer, 0)
    dgate_ref[0] = jnp.sum(jnp.where(hit, jnp.sum(sum_ref[...], axis=1, keepdims=True), 0.0), axis=0, keepdims=True)

    def combine(i, _):
        cols = pl.ds(pl.multiple_of(i * wide, wide), wide)
        out = dot(sel_back, yg_ref[:, cols], 1, 0)
        dx = dot(sel_back, dxe_ref[:, cols], 1, 0)
        if more:
            out += join_chunks(old_out_ref, cols).astype(F32)
            dx += join_chunks(old_dx_ref, cols).astype(F32)
        split_chunks(out_ref, cols, out)
        split_chunks(dx_ref, cols, dx)
        return 0

    lax.fori_loop(0, model // wide, combine, 0)


def run_expert(rank, gate, x, dz, w, old, capacity, wide=2048, narrow=1024):
    blocks, rows = rank.shape
    model, feed = x.shape[1], w.shape[1] // 3
    def per_block(r, c): return pl.BlockSpec((r, c), lambda i: (i, 0))
    line = pl.BlockSpec((1, 1, rows), lambda i: (i, 0, 0))
    shape = jax.ShapeDtypeStruct
    slots = blocks * capacity
    more = old is not None
    form, result = chunk_form(blocks, rows, model)
    return pl.pallas_call(
        functools.partial(expert_kernel, wide, narrow, more),
        grid=(blocks,),
        in_specs=[line, pl.BlockSpec((1, rows, 1), lambda i: (i, 0, 0)), line, per_block(rows, model), per_block(rows, model),
            pl.BlockSpec(w.shape, lambda i: (0, 0), pipeline_mode=pl.Buffered(1))] + [form] * (2 if more else 0),
        out_specs=[per_block(capacity, model), per_block(capacity, model), per_block(capacity, feed), per_block(capacity, 2 * feed), form, form, line],
        out_shape=[shape((slots, model), BF16), shape((slots, model), BF16), shape((slots, feed), BF16), shape((slots, 2 * feed), BF16),
            result, result, shape((blocks, 1, rows), F32)],
        scratch_shapes=[pltpu.VMEM((capacity, model), BF16)] * 3 + [pltpu.VMEM((capacity, 128), F32)],
        compiler_params=pltpu.CompilerParams(vmem_limit_bytes=VMEM_LIMIT),
        cost_estimate=BRIEF,
        name="expert",
    )(rank[:, None, :], rank[:, :, None], gate[:, None, :], x, dz, w, *(old or ()))


def weight_kernel(narrow, xg_ref, dy_ref, dgu_ref, hm_ref, out_ref, flip_ref):
    feed = hm_ref.shape[1]
    for src, other, base, width in ((xg_ref, dgu_ref, 0, 2 * feed), (dy_ref, hm_ref, 2 * feed, feed)):
        flip_ref[...] = src[...].T
        def step(i, _):
            cols = pl.ds(pl.multiple_of(i * narrow, narrow), narrow)
            to = pl.ds(pl.multiple_of(base + i * narrow, narrow), narrow)
            out_ref[:, to] = dot(flip_ref[...], other[:, cols], 1, 0).astype(BF16)
            return 0
        lax.fori_loop(0, width // narrow, step, 0)


def expert_weight_grad(xg, dy, dgu, hm, block=512, narrow=1024):
    slots, model = xg.shape
    feed = hm.shape[1]
    cut = pl.BlockSpec((slots, block), lambda i: (0, i))
    def whole(c): return pl.BlockSpec((slots, c), lambda i: (0, 0), pipeline_mode=pl.Buffered(1))
    return pl.pallas_call(
        functools.partial(weight_kernel, narrow),
        grid=(model // block,),
        in_specs=[cut, cut, whole(2 * feed), whole(feed)],
        out_specs=pl.BlockSpec((block, 3 * feed), lambda i: (i, 0)),
        out_shape=jax.ShapeDtypeStruct((model, 3 * feed), BF16),
        scratch_shapes=[pltpu.VMEM((block, slots), BF16)],
        compiler_params=pltpu.CompilerParams(vmem_limit_bytes=VMEM_LIMIT),
        cost_estimate=BRIEF,
        name="expert_weight_grad",
    )(xg, dy, dgu, hm)

def adam_kernel(rate, w_ref, g_ref, m_ref, v_ref, *refs):
    m_out, v_out, w_out = refs[-3:]
    new = adam_step(w_ref[0], g_ref[...], m_ref[0], v_ref[0], rate)
    m_out[0], v_out[0], w_out[0] = new

def adam_expert(e, weight, grad, first, second, old, rate, block=64):
    _, rows, cols = weight.shape
    one = pl.BlockSpec((1, block, cols), lambda i: (e, i, 0))
    out = jax.ShapeDtypeStruct(weight.shape, F32)
    old = tuple(old or ())
    return pl.pallas_call(
        functools.partial(adam_kernel, rate),
        grid=(rows // block,),
        in_specs=[one, pl.BlockSpec((block, cols), lambda i: (i, 0)), one, one] + [pl.BlockSpec(memory_space=pl.ANY)] * len(old),
        out_specs=[one] * 3,
        out_shape=[out] * 3,
        input_output_aliases={4 + i: i for i in range(len(old))},
        compiler_params=pltpu.CompilerParams(vmem_limit_bytes=VMEM_LIMIT),
        cost_estimate=BRIEF,
        name="adam_expert",
    )(weight, grad, first, second, *old)


def norm_back(dn, value, gain):
    scale = lax.rsqrt(jnp.mean(value * value, axis=-1, keepdims=True) + NORM_EPS)
    hat = value * scale
    inner = dn * gain
    back = scale * (inner - hat * jnp.mean(inner * hat, axis=-1, keepdims=True))
    return back, jnp.sum(dn * hat, axis=0)


def after(value, *others):
    return lax.optimization_barrier((value, *others))[0]


def body(
    tokens,
    cotangent,
    doc_lengths,
    routes,
    attn_weight,
    router_weight,
    gain_values,
    expert_weight,
    attn_first,
    attn_second,
    router_first,
    router_second,
    gain_first,
    gain_second,
    expert_first,
    expert_second,
):
    fsdp_count, seq_count = lax.axis_size("fsdp"), lax.axis_size("seq")
    everywhere = ("seq", "fsdp")
    here, plane = lax.axis_index("fsdp"), lax.axis_index("seq")
    around = here ^ jnp.arange(fsdp_count, dtype=jnp.int32)
    planes = plane ^ jnp.arange(seq_count, dtype=jnp.int32)
    rows, model = tokens.shape[1:]
    length = rows * seq_count
    experts = EXP_DEV * fsdp_count
    capacity = (rows * TOP // experts * 4 // 3 + 7) // 8 * 8
    width = model // fsdp_count
    shard = attn_weight.shape[0]
    members, chunk = fsdp_count // seq_count, rows // fsdp_count
    blocks = fsdp_count

    def blocked(parts):
        stacked = jnp.stack([part.reshape(blocks, chunk, -1) for part in parts], axis=1)
        return stacked.reshape(blocks * rows, -1)

    def pieces(value):
        cut = value.reshape(blocks, fsdp_count, chunk, -1)
        return [cut[:, k].reshape(rows, -1) for k in range(fsdp_count)]

    with jax.named_scope("gather_wo"):
        out_part = gather_direct(attn_weight[:, 3 * model :], "seq", seq_count)
    with jax.named_scope("remap_x"):
        x_low = to_plane(tokens[0], seq_count, fsdp_count)
    with jax.named_scope("gather_wqkv"):
        first_part = attn_weight[:, : 3 * model].reshape(shard, 3, fsdp_count, width).transpose(2, 0, 1, 3)
        first_part = reorder(first_part.reshape(fsdp_count, shard, 3 * width), around)
        first_part = reorder(jnp.stack(exchange(list(first_part), "fsdp", fsdp_count)), around)
        in_proj = lax.all_gather(first_part.reshape(fsdp_count * shard, 3 * width), "seq", axis=0, tiled=True)
    with jax.named_scope("gather_small"):
        flat = [router_weight.reshape(-1), gain_values, routes.reshape(-1), doc_lengths.reshape(-1)]
        sizes = [v.shape[0] for v in flat]
        starts = [sum(sizes[:i]) for i in range(len(sizes))]
        flat = after(jnp.concatenate([v.astype(F32) for v in flat]), x_low)
        flat = jnp.pad(flat, (0, -flat.shape[0] % 1024)).reshape(-1, 128)
        lines = flat.shape[0]
        small_all = lax.all_gather(flat, "seq", axis=0, tiled=True)
        small_all = lax.all_gather(small_all, "fsdp", axis=0, tiled=True)
        every = small_all.reshape(fsdp_count, seq_count, lines * 128)
        per_device = every.transpose(1, 0, 2).reshape(seq_count * fsdp_count, lines * 128)
        full_router = per_device[:, : sizes[0]].reshape(model, experts).astype(BF16)
        gains = per_device[:, starts[1] : starts[2]].reshape(-1)
        attn_gain, ffn_gain = gains[:model], gains[model : 2 * model]
        gain_q = gains[2 * model : 2 * model + HDIM][None]
        gain_k = gains[2 * model + HDIM : 2 * model + 2 * HDIM][None]
        meta = lax.dynamic_slice_in_dim(every, plane * members, members, 0)[:, :, starts[2] : starts[3] + 3]
        meta = meta.astype(jnp.int32)
    docs = meta[:, 0, rows * TOP : rows * TOP + 3]
    routes_all = meta[:, :, : rows * TOP].reshape(blocks, fsdp_count, chunk, TOP)
    routes_all = reorder(routes_all, around, 1).reshape(blocks, rows, TOP)
    positions = (
        jnp.arange(seq_count, dtype=jnp.int32)[:, None, None] * rows
        + around[None, :, None] * chunk
        + jnp.arange(chunk, dtype=jnp.int32)[None, None, :]
    ).reshape(1, length)
    doc_index = (positions >= docs[:, :1]).astype(jnp.int32) + (
        positions >= docs[:, :1] + docs[:, 1:2]
    ).astype(jnp.int32)
    row_doc, col_doc = doc_index[:, :, None], doc_index[:, None, :]
    frequency = ROPE_BASE ** (-jnp.arange(HDIM // 2, dtype=F32) / (HDIM // 2))
    angles = positions[0].astype(F32)[:, None] * frequency[None, :]
    cosine, sine = jnp.cos(angles), jnp.sin(angles)
    cosine = jnp.concatenate([cosine, cosine], axis=1)
    sine = jnp.concatenate([-sine, sine], axis=1)

    with jax.named_scope("gather_experts"):
        expert_later = after(expert_weight, first_part)
        expert_full = [lax.all_gather(expert_later[e], "seq", axis=0, tiled=True) for e in range(EXP_DEV)]
    with jax.named_scope("gather_wo"):
        out_part = jnp.stack(plane_gather(fsdp_count, out_part.reshape(seq_count * shard, model)))
        out_part = out_part.reshape(fsdp_count * seq_count, shard, model)
        place = jnp.arange(seq_count * fsdp_count, dtype=jnp.int32)
        place = (here ^ (place % fsdp_count)) * seq_count + (plane ^ (place // fsdp_count))
        out_proj = reorder(out_part, place).reshape(model, model)
    with jax.named_scope("gather_x"):
        x_all = blocked(plane_gather(fsdp_count, x_low))
    with jax.named_scope("remap_dz"):
        dz_low = to_plane(after(cotangent[0], x_all), seq_count, fsdp_count)

    own = here * EXP_DEV + jnp.arange(EXP_DEV, dtype=jnp.int32)
    named = jnp.any(routes_all[:, None, :, :] == own[None, :, None, None], axis=3)
    before = jnp.cumsum(named.astype(jnp.int32), axis=2) - named.astype(jnp.int32)
    rank = jnp.where(named, before, -1)
    chosen = jnp.any(
        routes_all[:, :, :, None] == jnp.arange(experts, dtype=jnp.int32)[None, None, None, :], axis=2
    )

    cosine_all, sine_all = jnp.tile(cosine, (members, 1)), jnp.tile(sine, (members, 1))
    a_all, q_low, k_low, v_low, q_pre, k_pre = project(
        x_all, attn_gain[None], in_proj, cosine_all, sine_all, gain_q, gain_k, rows
    )
    with jax.named_scope("gather_dz"):
        dz_all = blocked(plane_gather(fsdp_count, dz_low))
    seq_shape = (members, length, width)
    q_seq, k_seq, v_seq = (t.reshape(seq_shape) for t in (q_low, k_low, v_low))
    o_all = attend(q_seq, k_seq, v_seq, row_doc, col_doc)
    with jax.named_scope("o_exchange"):
        o_own = reorder(o_all.reshape(blocks, fsdp_count, chunk, width), around, 1)
        o_own = o_own.transpose(1, 0, 2, 3).reshape(fsdp_count, rows, width)
        o_own = lax.all_to_all(o_own, "fsdp", split_axis=0, concat_axis=0, tiled=True)
        o_own = o_own.transpose(1, 0, 2).reshape(rows, model)
    inputs = x_low.astype(F32)
    middle = inputs + dot(o_own, out_proj, 1, 0)
    middle_scale = lax.rsqrt(jnp.mean(middle * middle, axis=-1, keepdims=True) + NORM_EPS)
    normed = (middle * middle_scale * ffn_gain).astype(BF16)

    with jax.named_scope("gather_xn"):
        xn_all = blocked(plane_gather(fsdp_count, normed))
    with jax.named_scope("gates"):
        logits = dot(xn_all, full_router, 1, 0).reshape(blocks, rows, experts)
        top = jnp.max(jnp.where(chosen, logits, -jnp.inf), axis=2, keepdims=True)
        raised = jnp.where(chosen, jnp.exp(logits - top), 0.0)
        gates = raised / jnp.sum(raised, axis=2, keepdims=True)
        gates_mine = lax.dynamic_slice_in_dim(gates, here * EXP_DEV, EXP_DEV, axis=2)
    sums, gate_back, expert_share, held = None, [], [], None
    for e in range(EXP_DEV):
        with jax.named_scope(f"expert{e}"):
            w = expert_full[e] if held is None else after(expert_full[e], held)
            xg, dy, hm, dgu, mixed, dxn, dgate = run_expert(
                rank[:, e], gates_mine[:, :, e], xn_all, dz_all, w, sums, capacity
            )
            sums = (mixed, dxn)
            gate_back.append(dgate[:, 0])
            if e == EXP_DEV - 1:
                dxn = by_owner(dxn, blocks)
                dxn_first = scatter_first(fsdp_count, dxn)
                if dxn_first is not None:
                    xg = after(xg, dxn_first)
            held = expert_weight_grad(xg, dy, dgu, hm)
            expert_share.append(lax.psum_scatter(held, "seq", scatter_dimension=0, tiled=True))

    with jax.named_scope("router_back"):
        parts = exchange(pieces(jnp.stack(gate_back, axis=2)), "fsdp", fsdp_count)
        gate_grad = reorder(jnp.stack(parts, axis=1), around, 1).reshape(rows, experts)
        gates_own, chosen_own = pieces(gates)[0], pieces(chosen)[0]
        gate_grad = jnp.where(chosen_own, gate_grad, 0.0)
        dlog = (gates_own * (gate_grad - jnp.sum(gates_own * gate_grad, axis=1, keepdims=True))).astype(BF16)
    with jax.named_scope("scatter_dxn"):
        dxn_own = scatter_rest(fsdp_count, dxn, dxn_first)
    dxn_own = dxn_own + dot(dlog, full_router, 1, 1)
    middle_back, ffn_gain_grad = norm_back(dxn_own, middle, ffn_gain)
    middle_grad = dz_low.astype(F32) + middle_back
    db = middle_grad.astype(BF16)
    with jax.named_scope("do_exchange"):
        do_own = dot(db, out_proj, 1, 1).astype(BF16).reshape(rows, fsdp_count, width).transpose(1, 0, 2)
        do_own = lax.all_to_all(do_own, "fsdp", split_axis=0, concat_axis=0, tiled=True)
        do_all = reorder(do_own, around).reshape(fsdp_count, blocks, chunk, width).transpose(1, 0, 2, 3)
        do_all = do_all.reshape(seq_shape)
    do_all = after(do_all, held, expert_share[0])
    dq, dk, dv = (
        t.reshape(-1, width) for t in attend_back(q_seq, k_seq, v_seq, do_all, row_doc, col_doc)
    )
    with jax.named_scope("scatter_out"):
        mixture = plane_scatter(fsdp_count, by_owner(after(mixed, dq), blocks))
        layer_low = (middle + mixture).astype(BF16)
    d_proj, da_part, gain_qk = project_back(
        dq, dk, dv, q_pre, k_pre, cosine_all, sine_all, gain_q, gain_k, in_proj, rows
    )
    with jax.named_scope("remap_out"):
        layer_out = from_plane(layer_low, here, plane, seq_count, fsdp_count)
    with jax.named_scope("scatter_da"):
        da = plane_scatter(fsdp_count, by_owner(da_part, blocks))
    input_back, attn_gain_grad = norm_back(da, inputs, attn_gain)
    input_low = (middle_grad + input_back).astype(BF16)
    with jax.named_scope("scatter_wqkv"):
        in_grad = after(dot(a_all, d_proj, 0, 0).astype(BF16), expert_share[1], input_low)
        in_share = lax.psum_scatter(in_grad, "seq", scatter_dimension=0, tiled=True)
        in_share = reorder(in_share.reshape(fsdp_count, shard, 3 * width), around)
        in_share = reorder(jnp.stack(exchange(list(in_share), "fsdp", fsdp_count)), around)
        in_share = in_share.reshape(fsdp_count, shard, 3, width).transpose(1, 2, 0, 3).reshape(shard, 3 * model)
    with jax.named_scope("remap_grad"):
        input_grad = from_plane_whole(input_low, seq_count, fsdp_count).astype(F32)
    with jax.named_scope("scatter_wo"):
        out_grad = dot(o_own, db, 0, 0).astype(BF16).reshape(seq_count, fsdp_count, shard, model)
        pairs = reorder(around, jnp.arange(fsdp_count).reshape(-1, 2).T.reshape(-1))
        out_grad = reorder(out_grad, pairs, 1).transpose(1, 0, 2, 3)
        out_grad = out_grad.reshape(2, fsdp_count // 2, seq_count * shard, model)
        out_share = plane_scatter(fsdp_count, after(out_grad, da)).astype(BF16)
        out_share = reorder(out_share.reshape(seq_count, shard, model), planes)
        out_share = sum(p.astype(F32) for p in exchange(list(out_share), "seq", seq_count))
    with jax.named_scope("small_sum"):
        router_grad = dot(normed, dlog, 0, 0)
        small = jnp.concatenate(
            [router_grad.reshape(-1), attn_gain_grad, ffn_gain_grad, gain_qk[0], gain_qk[1]]
        )
        own_router, own_gain = shard * experts, gain_values.shape[0]

        def shares(value, p):
            device = p * fsdp_count + here
            return jnp.concatenate(
                [
                    lax.dynamic_slice_in_dim(value, device * own_router, own_router),
                    lax.dynamic_slice_in_dim(value, model * experts + device * own_gain, own_gain),
                ]
            )

        small = small_sum(small, shares, planes, seq_count, fsdp_count)
        router_share, gain_share = small[:own_router].reshape(shard, experts), small[own_router:]

    attn_share = jnp.concatenate([in_share.astype(F32), out_share], axis=1)
    attn_new = adam_step(attn_weight, attn_share, attn_first, attn_second, RATE_ATTN)
    router_new = adam_step(router_weight, router_share, router_first, router_second, RATE_ROUTER)
    gain_new = adam_step(gain_values, gain_share, gain_first, gain_second, RATE_GAIN)
    expert_new = None
    for e in range(EXP_DEV):
        expert_new = adam_expert(
            e, expert_weight, expert_share[e], expert_first, expert_second, expert_new, RATE_EXPERT
        )
    return (layer_out[None], input_grad[None], *attn_new, *router_new, *gain_new, *expert_new)


def solution(mesh):
    tokens = P("fsdp", "seq", None)
    matrix, vector = P(("seq", "fsdp"), None), P(("seq", "fsdp"))
    return jax.shard_map(
        body,
        mesh=mesh,
        in_specs=(
            tokens,
            tokens,
            P("fsdp", None),
            tokens,
            matrix,
            matrix,
            vector,
            tokens,
            matrix,
            matrix,
            matrix,
            matrix,
            vector,
            vector,
            tokens,
            tokens,
        ),
        out_specs=(
            tokens,
            tokens,
            matrix,
            matrix,
            matrix,
            matrix,
            matrix,
            matrix,
            vector,
            vector,
            vector,
            tokens,
            tokens,
            tokens,
        ),
        check_vma=False,
    )
```

```python
import functools
import math

import jax
import jax.numpy as jnp
from jax import lax
from jax.experimental import pallas as pl
from jax.experimental.pallas import tpu as pltpu
from jax.sharding import PartitionSpec as P

HEADS = 16
HDIM = 128
FFE = 1024
TOP = 8
EXP_DEV = 2
STEP = 10

NORM_EPS = 1e-06
ROPE_BASE = 10000.0
BETA_ONE = 0.9
BETA_TWO = 0.95
ADAM_EPS = 1e-08
WEIGHT_DECAY = 0.1
RATE_ATTN = 0.1
RATE_ROUTER = 0.03
RATE_GAIN = 0.5
RATE_EXPERT = 0.1
VMEM_LIMIT = 56 * 1024 * 1024

BRIEF = pl.CostEstimate(flops=1000, bytes_accessed=1000, transcendentals=0)


def lasting(us):
    return pl.CostEstimate(flops=int(us * 1e9), bytes_accessed=1000, transcendentals=0)


F32 = jnp.float32
BF16 = jnp.bfloat16


def dot(a, b, ca, cb):
    return lax.dot_general(a, b, (((ca,), (cb,)), ((), ())), preferred_element_type=F32)


def adam_step(weight, gradient, first_state, second, step_rate):
    gradient = gradient.astype(F32)
    first_new = BETA_ONE * first_state + (1.0 - BETA_ONE) * gradient
    second_new = BETA_TWO * second + (1.0 - BETA_TWO) * gradient * gradient
    first_hat = first_new / (1.0 - BETA_ONE**STEP)
    second_hat = second_new / (1.0 - BETA_TWO**STEP)
    master = weight.astype(F32) * (1.0 - step_rate * WEIGHT_DECAY) - step_rate * first_hat / (
        jnp.sqrt(second_hat) + ADAM_EPS
    )
    return first_new, second_new, master


def swap(value, step, axis, count):
    return lax.ppermute(value, axis, [(i, i ^ step) for i in range(count)])


def gather_direct(value, axis, count):
    return jnp.stack([value] + [swap(value, k, axis, count) for k in range(1, count)])


def exchange(parts, axis, count):
    return [parts[0]] + [swap(parts[k], k, axis, count) for k in range(1, count)]


def reorder(stacked, index, axis=0):
    return jnp.take(stacked, index, axis=axis, mode="clip")


def plane_gather(count, value):
    if count != 8:
        whole = lax.all_gather(value, "fsdp")
        mine = lax.axis_index("fsdp")
        return [lax.dynamic_index_in_dim(whole, mine ^ k, 0, False) for k in range(count)]
    go = functools.partial(swap, axis="fsdp", count=count)
    half = value.shape[0] // 2
    by_x, by_y = go(value, 2), go(value, 4)
    far = jnp.concatenate([go(by_x[:half], 4), go(by_y[half:], 2)], axis=0)
    return [value, go(value, 1), by_x, go(by_x, 1), by_y, go(by_y, 1), far, go(far, 1)]


class Scatter:
    def __init__(self, count, near, far, hold=()):
        self.count, self.near = count, near
        if count != 8:
            stacked = jnp.stack([near, far], axis=1).reshape(count, *near.shape[1:])
            stacked = reorder(stacked, lax.axis_index("fsdp") ^ jnp.arange(count))
            self.sum = lax.psum_scatter(stacked, "fsdp", scatter_dimension=0).astype(F32)
            self.got, self.sends, self.lasts = self.sum, (self.sum,), (self.sum,)
            return
        self.half = near.shape[1] // 2
        self.got = swap(far, 1, "fsdp", count)
        sends = (self.total(slice(1, None, 2), 0).astype(BF16), self.total(slice(2, None), 1).astype(BF16))
        if hold:
            sends = lax.optimization_barrier((*sends, *hold))[:2]
        self.sends = sends

    def total(self, index, part):
        rows = slice(self.half * part, self.half * (part + 1))
        return self.near[index, rows].astype(F32) + self.got[index, rows].astype(F32)

    def second(self, *beside):
        if self.count == 8:
            self.by_x = swap(self.sends[0], 2, "fsdp", self.count)
            self.by_y = swap(self.sends[1], 4, "fsdp", self.count)
            if beside:
                self.by_x, self.by_y = lax.optimization_barrier((self.by_x, self.by_y, *beside))[:2]
            self.lasts = (
                (self.total(2, 0) + self.by_x[1].astype(F32)).astype(BF16),
                (self.total(1, 1) + self.by_y[1].astype(F32)).astype(BF16),
            )
        return self

    def third(self, *beside):
        if self.count != 8:
            return self.sum
        y_last = swap(self.lasts[0], 4, "fsdp", self.count)
        x_last = swap(self.lasts[1], 2, "fsdp", self.count)
        if beside:
            y_last, x_last = lax.optimization_barrier((y_last, x_last, *beside))[:2]
        top = self.total(0, 0) + self.by_x[0].astype(F32) + y_last.astype(F32)
        low = self.total(0, 1) + self.by_y[0].astype(F32) + x_last.astype(F32)
        return jnp.concatenate([top, low], axis=0)


def plane_sum(value, fsdp_count):
    step = 1
    while step < fsdp_count:
        value = value + swap(value, step, "fsdp", fsdp_count)
        step *= 2
    return value


def to_plane_fsdp(value, fsdp_count):
    value = value.reshape(fsdp_count, -1, value.shape[1])
    return lax.all_to_all(value, "fsdp", split_axis=0, concat_axis=0, tiled=True)


def to_plane_seq(value, seq_count, fsdp_count):
    _, chunk, width = value.shape
    members = fsdp_count // seq_count
    value = value.reshape(seq_count, members * chunk, width)
    value = lax.all_to_all(value, "seq", split_axis=0, concat_axis=0, tiled=True)
    value = value.reshape(seq_count, members, chunk, width).transpose(1, 0, 2, 3)
    return value.reshape(fsdp_count * chunk, width)


def from_plane_seq(value, seq_count, fsdp_count):
    rows, width = value.shape
    members, chunk = fsdp_count // seq_count, rows // fsdp_count
    value = value.reshape(members, seq_count, chunk, width).transpose(1, 0, 2, 3)
    value = value.reshape(seq_count, members * chunk, width)
    return lax.all_to_all(value, "seq", split_axis=0, concat_axis=0, tiled=True).reshape(rows, width)


def from_plane_fsdp(value, fsdp_count):
    rows, width = value.shape
    value = value.reshape(fsdp_count, rows // fsdp_count, width)
    return lax.all_to_all(value, "fsdp", split_axis=0, concat_axis=0, tiled=True).reshape(rows, width)


def head_norm(value):
    return lax.rsqrt(jnp.mean(value * value, axis=-1, keepdims=True) + NORM_EPS)


def turn(value, cosine, sine):
    return value * cosine + pltpu.roll(value, HDIM // 2, 1) * sine


def project_kernel(
    heads, x_ref, gain_ref, w_ref, cos_ref, sin_ref, gq_ref, gk_ref, a_ref, q_ref, k_ref, v_ref, qp_ref, kp_ref
):
    x = x_ref[...].astype(F32)
    a = (x * head_norm(x) * gain_ref[...]).astype(BF16)
    a_ref[...] = a
    width = heads * HDIM
    cosine, sine = cos_ref[...], sin_ref[...]
    for n, (low_ref, pre_ref, g_ref) in enumerate(((q_ref, qp_ref, gq_ref), (k_ref, kp_ref, gk_ref))):
        part = dot(a, w_ref[:, n * width : (n + 1) * width], 1, 0)
        pre_ref[...] = part
        for h in range(heads):
            cols = slice(h * HDIM, (h + 1) * HDIM)
            one = part[:, cols]
            low_ref[:, cols] = turn(one * head_norm(one) * g_ref[...], cosine, sine).astype(BF16)
    v_ref[...] = dot(a, w_ref[:, 2 * width :], 1, 0).astype(BF16)


def project(x, gain, w, cosine, sine, gain_q, gain_k, block):
    rows, model = x.shape
    width = w.shape[1] // 3
    heads = width // HDIM

    def row(cols):
        return pl.BlockSpec((block, cols), lambda i: (i, 0))

    def whole(shape):
        return pl.BlockSpec(shape, lambda i: (0, 0))

    shape = jax.ShapeDtypeStruct
    return pl.pallas_call(
        functools.partial(project_kernel, heads),
        grid=(rows // block,),
        in_specs=[
            row(model),
            whole((1, model)),
            whole(w.shape),
            row(HDIM),
            row(HDIM),
            whole((1, HDIM)),
            whole((1, HDIM)),
        ],
        out_specs=[row(model), row(width), row(width), row(width), row(width), row(width)],
        out_shape=[
            shape((rows, model), BF16),
            shape((rows, width), BF16),
            shape((rows, width), BF16),
            shape((rows, width), BF16),
            shape((rows, width), F32),
            shape((rows, width), F32),
        ],
        compiler_params=pltpu.CompilerParams(vmem_limit_bytes=VMEM_LIMIT),
        cost_estimate=BRIEF,
        name="project",
    )(x, gain, w, cosine, sine, gain_q, gain_k)


SCORE = HDIM**-0.5


def probabilities(q, k, row_doc, col_doc):
    scores = dot(q, k, 1, 1) * (SCORE * math.log2(math.e))
    weight = jnp.where(row_doc == col_doc, jnp.exp2(scores), 0.0)
    return weight * (1.0 / jnp.sum(weight, axis=1, keepdims=True))


def attend_kernel(block, q_ref, k_ref, v_ref, rd_ref, cd_ref, o_ref):
    k, v = k_ref[0], v_ref[0]

    def step(i, _):
        rows = pl.ds(i * block, block)
        p = probabilities(q_ref[0, rows, :], k, rd_ref[0, rows, :], cd_ref[0])
        o_ref[0, rows, :] = dot(p.astype(BF16), v, 1, 0).astype(BF16)
        return 0

    lax.fori_loop(0, q_ref.shape[1] // block, step, 0)


def attend_back_kernel(block, q_ref, k_ref, v_ref, do_ref, rd_ref, cd_ref, dq_ref, dk_ref, dv_ref, sk_ref, sv_ref):
    k, v = k_ref[0], v_ref[0]
    sk_ref[...] = jnp.zeros_like(sk_ref)
    sv_ref[...] = jnp.zeros_like(sv_ref)

    def step(i, _):
        rows = pl.ds(i * block, block)
        q, do = q_ref[0, rows, :], do_ref[0, rows, :]
        p = probabilities(q, k, rd_ref[0, rows, :], cd_ref[0])
        dp = dot(do, v, 1, 1)
        ds = (p * (dp - jnp.sum(p * dp, axis=1, keepdims=True))).astype(BF16)
        dq_ref[0, rows, :] = (dot(ds, k, 1, 0) * SCORE).astype(BF16)
        sk_ref[...] += dot(ds, q, 0, 0)
        sv_ref[...] += dot(p.astype(BF16), do, 0, 0)
        return 0

    lax.fori_loop(0, q_ref.shape[1] // block, step, 0)
    dk_ref[0] = (sk_ref[...] * SCORE).astype(BF16)
    dv_ref[0] = sv_ref[...].astype(BF16)


def attention_specs(length, width):
    head = pl.BlockSpec((1, length, HDIM), lambda s, h: (s, 0, h))
    row_doc = pl.BlockSpec((1, length, 1), lambda s, h: (s, 0, 0))
    col_doc = pl.BlockSpec((1, 1, length), lambda s, h: (s, 0, 0))
    return head, row_doc, col_doc


def attend(q, k, v, row_doc, col_doc):
    seqs, length, width = q.shape
    head, rd, cd = attention_specs(length, width)
    pairs = seqs * (width // HDIM) * length * length
    return pl.pallas_call(
        functools.partial(attend_kernel, 256),
        grid=(seqs, width // HDIM),
        in_specs=[head, head, head, rd, cd],
        out_specs=head,
        out_shape=jax.ShapeDtypeStruct(q.shape, BF16),
        compiler_params=pltpu.CompilerParams(vmem_limit_bytes=VMEM_LIMIT),
        cost_estimate=BRIEF,
        name="attend",
    )(q, k, v, row_doc, col_doc)


def attend_back(q, k, v, do, row_doc, col_doc):
    seqs, length, width = q.shape
    head, rd, cd = attention_specs(length, width)
    pairs = seqs * (width // HDIM) * length * length
    out = jax.ShapeDtypeStruct(q.shape, BF16)
    return pl.pallas_call(
        functools.partial(attend_back_kernel, 256),
        grid=(seqs, width // HDIM),
        in_specs=[head, head, head, head, rd, cd],
        out_specs=[head, head, head],
        out_shape=[out, out, out],
        scratch_shapes=[pltpu.VMEM((length, HDIM), F32), pltpu.VMEM((length, HDIM), F32)],
        compiler_params=pltpu.CompilerParams(vmem_limit_bytes=VMEM_LIMIT),
        cost_estimate=lasting(40),
        name="attend_back",
    )(q, k, v, do, row_doc, col_doc)


def project_back_kernel(
    heads, dq_ref, dk_ref, dv_ref, qp_ref, kp_ref, cos_ref, sin_ref, gq_ref, gk_ref, w_ref, dp_ref, dg_ref, *da_refs
):
    cosine, sine = cos_ref[...], -sin_ref[...]
    width = heads * HDIM

    @pl.when(pl.program_id(0) == 0)
    def _():
        dg_ref[...] = jnp.zeros_like(dg_ref)

    for n, (d_ref, pre_ref, g_ref) in enumerate(((dq_ref, qp_ref, gq_ref), (dk_ref, kp_ref, gk_ref))):
        gain = g_ref[...]
        total = jnp.zeros((1, HDIM), F32)
        for h in range(heads):
            cols = slice(h * HDIM, (h + 1) * HDIM)
            dn = turn(d_ref[:, cols].astype(F32), cosine, sine)
            pre = pre_ref[:, cols]
            scale = head_norm(pre)
            hat = pre * scale
            total += jnp.sum(dn * hat, axis=0, keepdims=True)
            inner = dn * gain
            back = scale * (inner - hat * jnp.mean(inner * hat, axis=1, keepdims=True))
            dp_ref[:, n * width + h * HDIM : n * width + (h + 1) * HDIM] = back.astype(BF16)
        dg_ref[n : n + 1, :] += total
    dp_ref[:, 2 * width :] = dv_ref[...]
    split_chunks(da_refs, slice(None), dot(dp_ref[...], w_ref[...], 1, 1))


def project_back(dq, dk, dv, q_pre, k_pre, cosine, sine, gain_q, gain_k, w, block):
    rows, width = dq.shape
    model = w.shape[0]
    form, result = chunk_form(rows // block, block, model)
    heads = width // HDIM

    def row(cols):
        return pl.BlockSpec((block, cols), lambda i: (i, 0))

    def whole(shape):
        return pl.BlockSpec(shape, lambda i: (0, 0))

    shape = jax.ShapeDtypeStruct
    return pl.pallas_call(
        functools.partial(project_back_kernel, heads),
        grid=(rows // block,),
        in_specs=[row(width)] * 5
        + [row(HDIM), row(HDIM), whole((1, HDIM)), whole((1, HDIM)), whole(w.shape)],
        out_specs=[row(3 * width), whole((8, HDIM)), *form],
        out_shape=[shape((rows, 3 * width), BF16), shape((8, HDIM), F32), *result],
        compiler_params=pltpu.CompilerParams(vmem_limit_bytes=VMEM_LIMIT),
        cost_estimate=lasting(28),
        name="project_back",
    )(dq, dk, dv, q_pre, k_pre, cosine, sine, gain_q, gain_k, w)


def join_chunks(refs, cols):
    if len(refs) == 1:
        return refs[0][:, cols]
    half = refs[0].shape[0]
    return jnp.concatenate([refs[k % 2][k // 2, 0, :, cols] for k in range(2 * half)], axis=0)


def split_chunks(refs, cols, value):
    if len(refs) == 1:
        refs[0][:, cols] = value.astype(BF16)
        return
    half, _, chunk, _ = refs[0].shape
    for k in range(2 * half):
        refs[k % 2][k // 2, 0, :, cols] = value[k * chunk : (k + 1) * chunk].astype(BF16)


def chunk_form(blocks, rows, model):
    chunk = rows // blocks
    if chunk % 16:
        return [pl.BlockSpec((rows, model), lambda i: (i, 0))], [jax.ShapeDtypeStruct((blocks * rows, model), BF16)]
    spec = pl.BlockSpec((blocks // 2, 1, chunk, model), lambda i: (0, i, 0, 0))
    return [spec] * 2, [jax.ShapeDtypeStruct((blocks // 2, blocks, chunk, model), BF16)] * 2


def by_owner(parts, blocks):
    if len(parts) == 1:
        value = parts[0]
        rows, model = value.shape[0] // blocks, value.shape[1]
        value = value.reshape(blocks, blocks // 2, 2, rows // blocks, model).transpose(2, 1, 0, 3, 4)
        parts = list(value)
    return [part.reshape(blocks // 2, -1, part.shape[-1]) for part in parts]


def expert_kernel(wide, narrow, more, parts, rank_ref, rank_col_ref, gate_ref, x_ref, dz_ref, w_ref, *refs):
    if more:
        old_out, old_dx, refs = refs[:parts], refs[parts : 2 * parts], refs[2 * parts :]
    xg_ref, dy_ref, hm_ref, dgu_ref, *refs = refs
    out_refs, dx_refs = refs[:parts], refs[parts : 2 * parts]
    dgate_ref, dzg_ref, yg_ref, dxe_ref, sum_ref = refs[2 * parts :]
    rows, model = x_ref.shape
    capacity, feed = hm_ref.shape
    hit = rank_ref[0] == lax.broadcasted_iota(jnp.int32, (capacity, rows), 0)
    sel = hit.astype(F32).astype(BF16)
    sel_back = (rank_col_ref[0] == lax.broadcasted_iota(jnp.int32, (rows, capacity), 1)).astype(F32).astype(BF16)
    gate = jnp.sum(jnp.where(hit, gate_ref[0], 0.0), axis=1, keepdims=True)

    def dispatch(i, _):
        cols = pl.ds(pl.multiple_of(i * wide, wide), wide)
        xg_ref[:, cols] = dot(sel, x_ref[:, cols], 1, 0).astype(BF16)
        dz = dot(sel, dz_ref[:, cols], 1, 0)
        dzg_ref[:, cols] = dz.astype(BF16)
        dy_ref[:, cols] = (gate * dz).astype(BF16)
        return 0

    lax.fori_loop(0, model // wide, dispatch, 0)

    def inner(i, _):
        cols = pl.ds(pl.multiple_of(i * narrow, narrow), narrow)
        ups = pl.ds(pl.multiple_of(feed + i * narrow, narrow), narrow)
        downs = pl.ds(pl.multiple_of(2 * feed + i * narrow, narrow), narrow)
        g = dot(xg_ref[...], w_ref[:, cols], 1, 0)
        u = dot(xg_ref[...], w_ref[:, ups], 1, 0)
        dh = dot(dy_ref[...], w_ref[:, downs], 1, 0)
        sig = 1.0 / (1.0 + jnp.exp(-g))
        silu = g * sig
        hm_ref[:, cols] = (silu * u).astype(BF16)
        dgu_ref[:, cols] = (dh * u * (sig + silu * (1.0 - sig))).astype(BF16)
        dgu_ref[:, ups] = (dh * silu).astype(BF16)
        return 0

    lax.fori_loop(0, feed // narrow, inner, 0)
    sum_ref[...] = jnp.zeros_like(sum_ref)

    def outer(i, _):
        cols = pl.ds(pl.multiple_of(i * narrow, narrow), narrow)
        y = dot(hm_ref[...], w_ref[cols, 2 * feed :], 1, 1).astype(BF16).astype(F32)
        part = y * dzg_ref[:, cols].astype(F32)
        total = part[:, :128]
        for j in range(1, narrow // 128):
            total += part[:, j * 128 : (j + 1) * 128]
        sum_ref[...] += total
        yg_ref[:, cols] = (gate * y).astype(BF16)
        dxe_ref[:, cols] = dot(dgu_ref[...], w_ref[cols, : 2 * feed], 1, 1).astype(BF16)
        return 0

    lax.fori_loop(0, model // narrow, outer, 0)
    dgate_ref[0] = jnp.sum(jnp.where(hit, jnp.sum(sum_ref[...], axis=1, keepdims=True), 0.0), axis=0, keepdims=True)

    def combine(i, _):
        cols = pl.ds(pl.multiple_of(i * wide, wide), wide)
        out = dot(sel_back, yg_ref[:, cols], 1, 0)
        dx = dot(sel_back, dxe_ref[:, cols], 1, 0)
        if more:
            out += join_chunks(old_out, cols).astype(F32)
            dx += join_chunks(old_dx, cols).astype(F32)
        split_chunks(out_refs, cols, out)
        split_chunks(dx_refs, cols, dx)
        return 0

    lax.fori_loop(0, model // wide, combine, 0)


def run_expert(rank, gate, x, dz, w, old, capacity, wide=2048, narrow=1024):
    blocks, rows = rank.shape
    model, feed = x.shape[1], w.shape[1] // 3
    def per_block(r, c): return pl.BlockSpec((r, c), lambda i: (i, 0))
    line = pl.BlockSpec((1, 1, rows), lambda i: (i, 0, 0))
    shape = jax.ShapeDtypeStruct
    slots = blocks * capacity
    more = bool(old)
    form, result = chunk_form(blocks, rows, model)
    xg, dy, hm, dgu, *rest = pl.pallas_call(
        functools.partial(expert_kernel, wide, narrow, more, len(form)),
        grid=(blocks,),
        in_specs=[line, pl.BlockSpec((1, rows, 1), lambda i: (i, 0, 0)), line, per_block(rows, model), per_block(rows, model),
            pl.BlockSpec(w.shape, lambda i: (0, 0), pipeline_mode=pl.Buffered(1))] + form * (2 if more else 0),
        out_specs=[per_block(capacity, model), per_block(capacity, model), per_block(capacity, feed), per_block(capacity, 2 * feed), *form, *form, line],
        out_shape=[shape((slots, model), BF16), shape((slots, model), BF16), shape((slots, feed), BF16), shape((slots, 2 * feed), BF16),
            *result, *result, shape((blocks, 1, rows), F32)],
        scratch_shapes=[pltpu.VMEM((capacity, model), BF16)] * 3 + [pltpu.VMEM((capacity, 128), F32)],
        compiler_params=pltpu.CompilerParams(vmem_limit_bytes=VMEM_LIMIT),
        cost_estimate=BRIEF,
        name="expert",
    )(rank[:, None, :], rank[:, :, None], gate[:, None, :], x, dz, w, *old)
    return xg, dy, hm, dgu, rest[: len(form)], rest[len(form) : -1], rest[-1][:, 0]


def weight_kernel(narrow, xg_ref, dy_ref, dgu_ref, hm_ref, out_ref, flip_ref):
    feed = hm_ref.shape[1]
    for src, other, base, width in ((xg_ref, dgu_ref, 0, 2 * feed), (dy_ref, hm_ref, 2 * feed, feed)):
        flip_ref[...] = src[...].T
        def step(i, _):
            cols = pl.ds(pl.multiple_of(i * narrow, narrow), narrow)
            to = pl.ds(pl.multiple_of(base + i * narrow, narrow), narrow)
            out_ref[:, to] = dot(flip_ref[...], other[:, cols], 1, 0).astype(BF16)
            return 0
        lax.fori_loop(0, width // narrow, step, 0)


def expert_weight_grad(xg, dy, dgu, hm, block=512, narrow=1024):
    slots, model = xg.shape
    feed = hm.shape[1]
    cut = pl.BlockSpec((slots, block), lambda i: (0, i))
    def whole(c): return pl.BlockSpec((slots, c), lambda i: (0, 0), pipeline_mode=pl.Buffered(1))
    return pl.pallas_call(
        functools.partial(weight_kernel, narrow),
        grid=(model // block,),
        in_specs=[cut, cut, whole(2 * feed), whole(feed)],
        out_specs=pl.BlockSpec((block, 3 * feed), lambda i: (i, 0)),
        out_shape=jax.ShapeDtypeStruct((model, 3 * feed), BF16),
        scratch_shapes=[pltpu.VMEM((block, slots), BF16)],
        compiler_params=pltpu.CompilerParams(vmem_limit_bytes=VMEM_LIMIT),
        cost_estimate=BRIEF,
        name="expert_weight_grad",
    )(xg, dy, dgu, hm)

def adam_kernel(rate, w_ref, g_ref, m_ref, v_ref, *refs):
    m_out, v_out, w_out = refs[-3:]
    new = adam_step(w_ref[0], g_ref[...], m_ref[0], v_ref[0], rate)
    m_out[0], v_out[0], w_out[0] = new

def adam_expert(e, weight, grad, first, second, old, rate, block=64):
    _, rows, cols = weight.shape
    one = pl.BlockSpec((1, block, cols), lambda i: (e, i, 0))
    out = jax.ShapeDtypeStruct(weight.shape, F32)
    old = tuple(old or ())
    return pl.pallas_call(
        functools.partial(adam_kernel, rate),
        grid=(rows // block,),
        in_specs=[one, pl.BlockSpec((block, cols), lambda i: (i, 0)), one, one] + [pl.BlockSpec(memory_space=pl.ANY)] * len(old),
        out_specs=[one] * 3,
        out_shape=[out] * 3,
        input_output_aliases={4 + i: i for i in range(len(old))},
        compiler_params=pltpu.CompilerParams(vmem_limit_bytes=VMEM_LIMIT),
        cost_estimate=BRIEF,
        name="adam_expert",
    )(weight, grad, first, second, *old)


def norm_back(dn, value, gain):
    scale = lax.rsqrt(jnp.mean(value * value, axis=-1, keepdims=True) + NORM_EPS)
    hat = value * scale
    inner = dn * gain
    back = scale * (inner - hat * jnp.mean(inner * hat, axis=-1, keepdims=True))
    return back, jnp.sum(dn * hat, axis=0)


def after(value, *others):
    return lax.optimization_barrier((value, *others))[0]


def body(
    tokens,
    cotangent,
    doc_lengths,
    routes,
    attn_weight,
    router_weight,
    gain_values,
    expert_weight,
    attn_first,
    attn_second,
    router_first,
    router_second,
    gain_first,
    gain_second,
    expert_first,
    expert_second,
):
    fsdp_count, seq_count = lax.axis_size("fsdp"), lax.axis_size("seq")
    everywhere = ("seq", "fsdp")
    here, plane = lax.axis_index("fsdp"), lax.axis_index("seq")
    around = here ^ jnp.arange(fsdp_count, dtype=jnp.int32)
    planes = plane ^ jnp.arange(seq_count, dtype=jnp.int32)
    rows, model = tokens.shape[1:]
    length = rows * seq_count
    experts = EXP_DEV * fsdp_count
    capacity = (rows * TOP // experts * 4 // 3 + 7) // 8 * 8
    width = model // fsdp_count
    shard = attn_weight.shape[0]
    members, chunk = fsdp_count // seq_count, rows // fsdp_count
    blocks = fsdp_count

    def blocked(parts):
        stacked = jnp.stack([part.reshape(blocks, chunk, -1) for part in parts], axis=1)
        return stacked.reshape(blocks * rows, -1)

    def pieces(value):
        cut = value.reshape(blocks, fsdp_count, chunk, -1)
        return [cut[:, k].reshape(rows, -1) for k in range(fsdp_count)]

    with jax.named_scope("gather_wo"):
        out_part = gather_direct(attn_weight[:, 3 * model :], "seq", seq_count)
    with jax.named_scope("remap_x"):
        x_low = to_plane_seq(to_plane_fsdp(tokens[0], fsdp_count), seq_count, fsdp_count)
    with jax.named_scope("gather_wqkv"):
        first_part = attn_weight[:, : 3 * model].reshape(shard, 3, fsdp_count, width).transpose(2, 0, 1, 3)
        first_part = reorder(first_part.reshape(fsdp_count, shard, 3 * width), around)
        first_part = reorder(jnp.stack(exchange(list(first_part), "fsdp", fsdp_count)), around)
        in_proj = lax.all_gather(first_part.reshape(fsdp_count * shard, 3 * width), "seq", axis=0, tiled=True)
    with jax.named_scope("gather_small"):
        flat = [router_weight.reshape(-1), gain_values, routes.reshape(-1), doc_lengths.reshape(-1)]
        sizes = [v.shape[0] for v in flat]
        starts = [sum(sizes[:i]) for i in range(len(sizes))]
        flat = after(jnp.concatenate([v.astype(F32) for v in flat]), x_low)
        flat = jnp.pad(flat, (0, -flat.shape[0] % 1024)).reshape(-1, 128)
        lines = flat.shape[0]
        small_all = lax.all_gather(flat, "seq", axis=0, tiled=True)
        small_all = lax.all_gather(small_all, "fsdp", axis=0, tiled=True)
        every = small_all.reshape(fsdp_count, seq_count, lines * 128)
        per_device = every.transpose(1, 0, 2).reshape(seq_count * fsdp_count, lines * 128)
        full_router = per_device[:, : sizes[0]].reshape(model, experts).astype(BF16)
        gains = per_device[:, starts[1] : starts[2]].reshape(-1)
        attn_gain, ffn_gain = gains[:model], gains[model : 2 * model]
        gain_q = gains[2 * model : 2 * model + HDIM][None]
        gain_k = gains[2 * model + HDIM : 2 * model + 2 * HDIM][None]
        meta = lax.dynamic_slice_in_dim(every, plane * members, members, 0)[:, :, starts[2] : starts[3] + 3]
        meta = meta.astype(jnp.int32)
    docs = meta[:, 0, rows * TOP : rows * TOP + 3]
    routes_all = meta[:, :, : rows * TOP].reshape(blocks, fsdp_count, chunk, TOP)
    routes_all = reorder(routes_all, around, 1).reshape(blocks, rows, TOP)
    positions = (
        jnp.arange(seq_count, dtype=jnp.int32)[:, None, None] * rows
        + around[None, :, None] * chunk
        + jnp.arange(chunk, dtype=jnp.int32)[None, None, :]
    ).reshape(1, length)
    doc_index = (positions >= docs[:, :1]).astype(jnp.int32) + (
        positions >= docs[:, :1] + docs[:, 1:2]
    ).astype(jnp.int32)
    row_doc, col_doc = doc_index[:, :, None], doc_index[:, None, :]
    frequency = ROPE_BASE ** (-jnp.arange(HDIM // 2, dtype=F32) / (HDIM // 2))
    angles = positions[0].astype(F32)[:, None] * frequency[None, :]
    cosine, sine = jnp.cos(angles), jnp.sin(angles)
    cosine = jnp.concatenate([cosine, cosine], axis=1)
    sine = jnp.concatenate([-sine, sine], axis=1)

    with jax.named_scope("gather_experts"):
        expert_later = after(expert_weight, first_part)
        expert_full = [lax.all_gather(expert_later[e], "seq", axis=0, tiled=True) for e in range(EXP_DEV)]
    with jax.named_scope("gather_wo"):
        out_part = jnp.stack(plane_gather(fsdp_count, out_part.reshape(seq_count * shard, model)))
        out_part = out_part.reshape(fsdp_count * seq_count, shard, model)
        place = jnp.arange(seq_count * fsdp_count, dtype=jnp.int32)
        place = (here ^ (place % fsdp_count)) * seq_count + (plane ^ (place // fsdp_count))
        out_proj = reorder(out_part, place).reshape(model, model)
    with jax.named_scope("gather_x"):
        x_all = blocked(plane_gather(fsdp_count, x_low))
    with jax.named_scope("remap_dz"):
        dz_low = to_plane_seq(to_plane_fsdp(after(cotangent[0], x_all), fsdp_count), seq_count, fsdp_count)

    own = here * EXP_DEV + jnp.arange(EXP_DEV, dtype=jnp.int32)
    named = jnp.any(routes_all[:, None, :, :] == own[None, :, None, None], axis=3)
    before = jnp.cumsum(named.astype(jnp.int32), axis=2) - named.astype(jnp.int32)
    rank = jnp.where(named, before, -1)
    chosen = jnp.any(
        routes_all[:, :, :, None] == jnp.arange(experts, dtype=jnp.int32)[None, None, None, :], axis=2
    )

    cosine_all, sine_all = jnp.tile(cosine, (members, 1)), jnp.tile(sine, (members, 1))
    a_all, q_low, k_low, v_low, q_pre, k_pre = project(
        x_all, attn_gain[None], in_proj, cosine_all, sine_all, gain_q, gain_k, rows
    )
    with jax.named_scope("gather_dz"):
        dz_all = blocked(plane_gather(fsdp_count, dz_low))
    seq_shape = (members, length, width)
    q_seq, k_seq, v_seq = (t.reshape(seq_shape) for t in (q_low, k_low, v_low))
    o_all = attend(q_seq, k_seq, v_seq, row_doc, col_doc)
    with jax.named_scope("o_exchange"):
        o_own = reorder(o_all.reshape(blocks, fsdp_count, chunk, width), around, 1)
        o_own = o_own.transpose(1, 0, 2, 3).reshape(fsdp_count, rows, width)
        o_own = lax.all_to_all(o_own, "fsdp", split_axis=0, concat_axis=0, tiled=True)
        o_own = o_own.transpose(1, 0, 2).reshape(rows, model)
    inputs = x_low.astype(F32)
    middle = inputs + dot(o_own, out_proj, 1, 0)
    middle_scale = lax.rsqrt(jnp.mean(middle * middle, axis=-1, keepdims=True) + NORM_EPS)
    normed = (middle * middle_scale * ffn_gain).astype(BF16)

    with jax.named_scope("gather_xn"):
        xn_all = blocked(plane_gather(fsdp_count, normed))
    with jax.named_scope("gates"):
        logits = dot(xn_all, full_router, 1, 0).reshape(blocks, rows, experts)
        top = jnp.max(jnp.where(chosen, logits, -jnp.inf), axis=2, keepdims=True)
        raised = jnp.where(chosen, jnp.exp(logits - top), 0.0)
        gates = raised / jnp.sum(raised, axis=2, keepdims=True)
        gates_mine = lax.dynamic_slice_in_dim(gates, here * EXP_DEV, EXP_DEV, axis=2)
    sums, gate_back, expert_share, held = (), [], [], None
    for e in range(EXP_DEV):
        with jax.named_scope(f"expert{e}"):
            w = expert_full[e] if held is None else after(expert_full[e], held)
            xg, dy, hm, dgu, mixed, dxn, dgate = run_expert(
                rank[:, e], gates_mine[:, :, e], xn_all, dz_all, w, sums, capacity
            )
            sums = (*mixed, *dxn)
            gate_back.append(dgate)
            if e == EXP_DEV - 1:
                gate_parts = exchange(pieces(jnp.stack(gate_back, axis=2)), "fsdp", fsdp_count)
                dxn = Scatter(fsdp_count, *by_owner(dxn, blocks), hold=gate_parts)
                xg = after(xg, *dxn.sends)
            held = expert_weight_grad(xg, dy, dgu, hm)
            expert_share.append(lax.psum_scatter(held, "seq", scatter_dimension=0, tiled=True))

    with jax.named_scope("router_back"):
        gate_grad = reorder(jnp.stack(gate_parts, axis=1), around, 1).reshape(rows, experts)
        gates_own, chosen_own = pieces(gates)[0], pieces(chosen)[0]
        gate_grad = jnp.where(chosen_own, gate_grad, 0.0)
        dlog = (gates_own * (gate_grad - jnp.sum(gates_own * gate_grad, axis=1, keepdims=True))).astype(BF16)
    with jax.named_scope("scatter_dxn"):
        dxn_own = dxn.second(held).third()
    dxn_own = dxn_own + dot(dlog, full_router, 1, 1)
    middle_back, ffn_gain_grad = norm_back(dxn_own, middle, ffn_gain)
    middle_grad = dz_low.astype(F32) + middle_back
    db = middle_grad.astype(BF16)

    with jax.named_scope("do_exchange"):
        do_own = dot(db, out_proj, 1, 1).astype(BF16).reshape(rows, fsdp_count, width).transpose(1, 0, 2)
        do_own = lax.all_to_all(do_own, "fsdp", split_axis=0, concat_axis=0, tiled=True)
        do_all = reorder(do_own, around).reshape(fsdp_count, blocks, chunk, width).transpose(1, 0, 2, 3)
        do_all = do_all.reshape(seq_shape)
    with jax.named_scope("scatter_out"):
        near, far = by_owner(mixed, blocks)
        mixed = Scatter(fsdp_count, near, after(far, db), hold=(do_all,))
    do_all = after(do_all, expert_share[0], *mixed.sends)
    dq, dk, dv = (
        t.reshape(-1, width) for t in attend_back(q_seq, k_seq, v_seq, do_all, row_doc, col_doc)
    )
    with jax.named_scope("scatter_out"):
        mixed = mixed.second(dq)
    d_proj, gain_qk, *da_part = project_back(
        after(dq, *mixed.lasts), dk, dv, q_pre, k_pre, cosine_all, sine_all, gain_q, gain_k, in_proj, rows
    )
    with jax.named_scope("scatter_out"):
        layer_low = (middle + mixed.third(d_proj)).astype(BF16)
    with jax.named_scope("scatter_da"):
        near, far = by_owner(da_part, blocks)
        da = Scatter(fsdp_count, near, after(far, layer_low))
    with jax.named_scope("remap_out"):
        layer_out = from_plane_seq(layer_low, seq_count, fsdp_count)
    with jax.named_scope("weight_grads"):
        in_grad = dot(after(a_all, *da.sends), d_proj, 0, 0).astype(BF16)
        expert_new = adam_expert(
            0, expert_weight, after(expert_share[0], *da.sends), expert_first, expert_second, None, RATE_EXPERT
        )
    with jax.named_scope("scatter_da"):
        da = da.second(in_grad, expert_new[0])
    with jax.named_scope("weight_grads"):
        out_grad = dot(after(o_own, *da.lasts), db, 0, 0).astype(BF16)
        out_grad = out_grad.reshape(seq_count, fsdp_count, shard, model)
        pairs = reorder(around, jnp.arange(fsdp_count).reshape(-1, 2).T.reshape(-1))
        out_grad = reorder(out_grad, pairs, 1).transpose(1, 0, 2, 3)
        out_grad = out_grad.reshape(2, fsdp_count // 2, seq_count * shard, model)
    with jax.named_scope("scatter_da"):
        da_own = da.third(out_grad, layer_out)
    input_back, attn_gain_grad = norm_back(da_own, inputs, attn_gain)
    input_low = (middle_grad + input_back).astype(BF16)
    with jax.named_scope("remap_grad"):
        input_grad = from_plane_seq(input_low, seq_count, fsdp_count)
    with jax.named_scope("scatter_wqkv"):
        in_grad = after(in_grad, input_low)
        in_share = lax.psum_scatter(in_grad, "seq", scatter_dimension=0, tiled=True)
    with jax.named_scope("small_sum"):
        router_grad = dot(normed, dlog, 0, 0)
        small = jnp.concatenate(
            [router_grad.reshape(-1), attn_gain_grad, ffn_gain_grad, gain_qk[0], gain_qk[1]]
        )
        small = plane_sum(small, fsdp_count)
        own_router, own_gain = shard * experts, gain_values.shape[0]

        def own_part(p):
            device = p * fsdp_count + here
            return jnp.concatenate(
                [
                    lax.dynamic_slice_in_dim(small, device * own_router, own_router),
                    lax.dynamic_slice_in_dim(small, model * experts + device * own_gain, own_gain),
                ]
            )

        small_parts = [own_part(planes[m]) for m in range(seq_count)]
    with jax.named_scope("scatter_wo"):
        out_grad = Scatter(fsdp_count, out_grad[0], after(out_grad[1], input_low), hold=small_parts)
    with jax.named_scope("small_sum"):
        small_parts = exchange(small_parts, "seq", seq_count)
    for e in range(1, EXP_DEV):
        expert_new = adam_expert(
            e,
            expert_weight,
            after(expert_share[e], *out_grad.sends),
            expert_first,
            expert_second,
            expert_new,
            RATE_EXPERT,
        )
    with jax.named_scope("scatter_wo"):
        out_grad = out_grad.second(expert_new[0])
        out_share = out_grad.third().astype(BF16)
    with jax.named_scope("scatter_wo"):
        out_parts = reorder(out_share.reshape(seq_count, shard, model), planes)
        out_parts = exchange(list(out_parts), "seq", seq_count)
    with jax.named_scope("scatter_wqkv"):
        in_share, *waiting = lax.optimization_barrier((in_share, *out_parts, *small_parts))
        in_share = reorder(in_share.reshape(fsdp_count, shard, 3 * width), around)
        in_share = reorder(jnp.stack(exchange(list(in_share), "fsdp", fsdp_count)), around)
        in_share = in_share.reshape(fsdp_count, shard, 3, width).transpose(1, 2, 0, 3).reshape(shard, 3 * model)
    with jax.named_scope("remap"):
        both = jnp.concatenate([input_grad, layer_out], axis=1)
        both = from_plane_fsdp(after(both, *out_grad.lasts), fsdp_count)
        input_grad, layer_out = both[:, :model].astype(F32), both[:, model:]
    out_share = sum(p.astype(F32) for p in waiting[:seq_count])
    small_own = sum(waiting[seq_count:])
    router_share, gain_share = small_own[:own_router].reshape(shard, experts), small_own[own_router:]

    attn_share = jnp.concatenate([in_share.astype(F32), out_share], axis=1)
    attn_new = adam_step(attn_weight, attn_share, attn_first, attn_second, RATE_ATTN)
    router_new = adam_step(router_weight, router_share, router_first, router_second, RATE_ROUTER)
    gain_new = adam_step(gain_values, gain_share, gain_first, gain_second, RATE_GAIN)
    return (layer_out[None], input_grad[None], *attn_new, *router_new, *gain_new, *expert_new)


def solution(mesh):
    tokens = P("fsdp", "seq", None)
    matrix, vector = P(("seq", "fsdp"), None), P(("seq", "fsdp"))
    return jax.shard_map(
        body,
        mesh=mesh,
        in_specs=(
            tokens,
            tokens,
            P("fsdp", None),
            tokens,
            matrix,
            matrix,
            vector,
            tokens,
            matrix,
            matrix,
            matrix,
            matrix,
            vector,
            vector,
            tokens,
            tokens,
        ),
        out_specs=(
            tokens,
            tokens,
            matrix,
            matrix,
            matrix,
            matrix,
            matrix,
            matrix,
            vector,
            vector,
            vector,
            tokens,
            tokens,
            tokens,
        ),
        check_vma=False,
    )
```

```python
import functools
import math

import jax
import jax.numpy as jnp
from jax import lax
from jax.experimental import pallas as pl
from jax.experimental.pallas import tpu as pltpu
from jax.sharding import PartitionSpec as P

HEADS = 16
HDIM = 128
FFE = 1024
TOP = 8
EXP_DEV = 2
STEP = 10

NORM_EPS = 1e-06
ROPE_BASE = 10000.0
BETA_ONE = 0.9
BETA_TWO = 0.95
ADAM_EPS = 1e-08
WEIGHT_DECAY = 0.1
RATE_ATTN = 0.1
RATE_ROUTER = 0.03
RATE_GAIN = 0.5
RATE_EXPERT = 0.1
VMEM_LIMIT = 56 * 1024 * 1024

BRIEF = pl.CostEstimate(flops=1000, bytes_accessed=1000, transcendentals=0)


def lasting(us):
    return pl.CostEstimate(flops=int(us * 1e9), bytes_accessed=1000, transcendentals=0)


F32 = jnp.float32
BF16 = jnp.bfloat16


def dot(a, b, ca, cb):
    return lax.dot_general(a, b, (((ca,), (cb,)), ((), ())), preferred_element_type=F32)


def adam_step(weight, gradient, first_state, second, step_rate):
    gradient = gradient.astype(F32)
    first_new = BETA_ONE * first_state + (1.0 - BETA_ONE) * gradient
    second_new = BETA_TWO * second + (1.0 - BETA_TWO) * gradient * gradient
    first_hat = first_new / (1.0 - BETA_ONE**STEP)
    second_hat = second_new / (1.0 - BETA_TWO**STEP)
    master = weight.astype(F32) * (1.0 - step_rate * WEIGHT_DECAY) - step_rate * first_hat / (
        jnp.sqrt(second_hat) + ADAM_EPS
    )
    return first_new, second_new, master


def swap(value, step, axis, count):
    return lax.ppermute(value, axis, [(i, i ^ step) for i in range(count)])


def gather_direct(value, axis, count):
    return jnp.stack([value] + [swap(value, k, axis, count) for k in range(1, count)])


def exchange(parts, axis, count):
    return [parts[0]] + [swap(parts[k], k, axis, count) for k in range(1, count)]


def reorder(stacked, index, axis=0):
    return jnp.take(stacked, index, axis=axis, mode="clip")


def plane_gather(count, value):
    if count != 8:
        whole = lax.all_gather(value, "fsdp")
        mine = lax.axis_index("fsdp")
        return [lax.dynamic_index_in_dim(whole, mine ^ k, 0, False) for k in range(count)]
    go = functools.partial(swap, axis="fsdp", count=count)
    half = value.shape[0] // 2
    by_x, by_y = go(value, 2), go(value, 4)
    far = jnp.concatenate([go(by_x[:half], 4), go(by_y[half:], 2)], axis=0)
    return [value, go(value, 1), by_x, go(by_x, 1), by_y, go(by_y, 1), far, go(far, 1)]


class Scatter:
    def __init__(self, count, near, far, hold=()):
        self.count, self.near = count, near
        if count != 8:
            stacked = jnp.stack([near, far], axis=1).reshape(count, *near.shape[1:])
            stacked = reorder(stacked, lax.axis_index("fsdp") ^ jnp.arange(count))
            self.sum = lax.psum_scatter(stacked, "fsdp", scatter_dimension=0).astype(F32)
            self.got, self.sends, self.lasts = self.sum, (self.sum,), (self.sum,)
            return
        self.half = near.shape[1] // 2
        self.got = swap(far, 1, "fsdp", count)
        sends = (self.total(slice(1, None, 2), 0).astype(BF16), self.total(slice(2, None), 1).astype(BF16))
        if hold:
            sends = lax.optimization_barrier((*sends, *hold))[:2]
        self.sends = sends

    def total(self, index, part):
        rows = slice(self.half * part, self.half * (part + 1))
        return self.near[index, rows].astype(F32) + self.got[index, rows].astype(F32)

    def second(self, *beside):
        if self.count == 8:
            self.by_x = swap(self.sends[0], 2, "fsdp", self.count)
            self.by_y = swap(self.sends[1], 4, "fsdp", self.count)
            if beside:
                self.by_x, self.by_y = lax.optimization_barrier((self.by_x, self.by_y, *beside))[:2]
            self.lasts = (
                (self.total(2, 0) + self.by_x[1].astype(F32)).astype(BF16),
                (self.total(1, 1) + self.by_y[1].astype(F32)).astype(BF16),
            )
        return self

    def third(self, *beside):
        if self.count != 8:
            return self.sum
        y_last = swap(self.lasts[0], 4, "fsdp", self.count)
        x_last = swap(self.lasts[1], 2, "fsdp", self.count)
        if beside:
            y_last, x_last = lax.optimization_barrier((y_last, x_last, *beside))[:2]
        top = self.total(0, 0) + self.by_x[0].astype(F32) + y_last.astype(F32)
        low = self.total(0, 1) + self.by_y[0].astype(F32) + x_last.astype(F32)
        return jnp.concatenate([top, low], axis=0)


def plane_sum(value, fsdp_count):
    step = 1
    while step < fsdp_count:
        value = value + swap(value, step, "fsdp", fsdp_count)
        step *= 2
    return value


def to_plane_fsdp(value, fsdp_count):
    value = value.reshape(fsdp_count, -1, value.shape[1])
    return lax.all_to_all(value, "fsdp", split_axis=0, concat_axis=0, tiled=True)


def to_plane_seq(value, seq_count, fsdp_count):
    _, chunk, width = value.shape
    members = fsdp_count // seq_count
    value = value.reshape(seq_count, members * chunk, width)
    value = lax.all_to_all(value, "seq", split_axis=0, concat_axis=0, tiled=True)
    value = value.reshape(seq_count, members, chunk, width).transpose(1, 0, 2, 3)
    return value.reshape(fsdp_count * chunk, width)


def from_plane_seq(value, seq_count, fsdp_count):
    rows, width = value.shape
    members, chunk = fsdp_count // seq_count, rows // fsdp_count
    value = value.reshape(members, seq_count, chunk, width).transpose(1, 0, 2, 3)
    value = value.reshape(seq_count, members * chunk, width)
    return lax.all_to_all(value, "seq", split_axis=0, concat_axis=0, tiled=True).reshape(rows, width)


def from_plane_fsdp(value, fsdp_count):
    rows, width = value.shape
    value = value.reshape(fsdp_count, rows // fsdp_count, width)
    return lax.all_to_all(value, "fsdp", split_axis=0, concat_axis=0, tiled=True).reshape(rows, width)


def head_norm(value):
    return lax.rsqrt(jnp.mean(value * value, axis=-1, keepdims=True) + NORM_EPS)


def turn(value, cosine, sine):
    return value * cosine + pltpu.roll(value, HDIM // 2, 1) * sine


def project_kernel(
    heads, x_ref, gain_ref, w_ref, cos_ref, sin_ref, gq_ref, gk_ref, a_ref, q_ref, k_ref, v_ref, qp_ref, kp_ref
):
    x = x_ref[...].astype(F32)
    a = (x * head_norm(x) * gain_ref[...]).astype(BF16)
    a_ref[...] = a
    width = heads * HDIM
    cosine, sine = cos_ref[...], sin_ref[...]
    for n, (low_ref, pre_ref, g_ref) in enumerate(((q_ref, qp_ref, gq_ref), (k_ref, kp_ref, gk_ref))):
        part = dot(a, w_ref[:, n * width : (n + 1) * width], 1, 0)
        pre_ref[...] = part
        for h in range(heads):
            cols = slice(h * HDIM, (h + 1) * HDIM)
            one = part[:, cols]
            low_ref[:, cols] = turn(one * head_norm(one) * g_ref[...], cosine, sine).astype(BF16)
    v_ref[...] = dot(a, w_ref[:, 2 * width :], 1, 0).astype(BF16)


def project(x, gain, w, cosine, sine, gain_q, gain_k, block):
    rows, model = x.shape
    width = w.shape[1] // 3
    heads = width // HDIM

    def row(cols):
        return pl.BlockSpec((block, cols), lambda i: (i, 0))

    def whole(shape):
        return pl.BlockSpec(shape, lambda i: (0, 0))

    shape = jax.ShapeDtypeStruct
    return pl.pallas_call(
        functools.partial(project_kernel, heads),
        grid=(rows // block,),
        in_specs=[
            row(model),
            whole((1, model)),
            whole(w.shape),
            row(HDIM),
            row(HDIM),
            whole((1, HDIM)),
            whole((1, HDIM)),
        ],
        out_specs=[row(model), row(width), row(width), row(width), row(width), row(width)],
        out_shape=[
            shape((rows, model), BF16),
            shape((rows, width), BF16),
            shape((rows, width), BF16),
            shape((rows, width), BF16),
            shape((rows, width), F32),
            shape((rows, width), F32),
        ],
        compiler_params=pltpu.CompilerParams(vmem_limit_bytes=VMEM_LIMIT),
        cost_estimate=BRIEF,
        name="project",
    )(x, gain, w, cosine, sine, gain_q, gain_k)


SCORE = HDIM**-0.5


def probabilities(q, k, row_doc, col_doc):
    scores = dot(q, k, 1, 1) * (SCORE * math.log2(math.e))
    weight = jnp.where(row_doc == col_doc, jnp.exp2(scores), 0.0)
    return weight * (1.0 / jnp.sum(weight, axis=1, keepdims=True))


def attend_kernel(block, q_ref, k_ref, v_ref, rd_ref, cd_ref, o_ref):
    k, v = k_ref[0], v_ref[0]

    def step(i, _):
        rows = pl.ds(i * block, block)
        p = probabilities(q_ref[0, rows, :], k, rd_ref[0, rows, :], cd_ref[0])
        o_ref[0, rows, :] = dot(p.astype(BF16), v, 1, 0).astype(BF16)
        return 0

    lax.fori_loop(0, q_ref.shape[1] // block, step, 0)


def attend_back_kernel(block, q_ref, k_ref, v_ref, do_ref, rd_ref, cd_ref, dq_ref, dk_ref, dv_ref, sk_ref, sv_ref):
    k, v = k_ref[0], v_ref[0]
    sk_ref[...] = jnp.zeros_like(sk_ref)
    sv_ref[...] = jnp.zeros_like(sv_ref)

    def step(i, _):
        rows = pl.ds(i * block, block)
        q, do = q_ref[0, rows, :], do_ref[0, rows, :]
        p = probabilities(q, k, rd_ref[0, rows, :], cd_ref[0])
        dp = dot(do, v, 1, 1)
        ds = (p * (dp - jnp.sum(p * dp, axis=1, keepdims=True))).astype(BF16)
        dq_ref[0, rows, :] = (dot(ds, k, 1, 0) * SCORE).astype(BF16)
        sk_ref[...] += dot(ds, q, 0, 0)
        sv_ref[...] += dot(p.astype(BF16), do, 0, 0)
        return 0

    lax.fori_loop(0, q_ref.shape[1] // block, step, 0)
    dk_ref[0] = (sk_ref[...] * SCORE).astype(BF16)
    dv_ref[0] = sv_ref[...].astype(BF16)


def attention_specs(length, width):
    head = pl.BlockSpec((1, length, HDIM), lambda s, h: (s, 0, h))
    row_doc = pl.BlockSpec((1, length, 1), lambda s, h: (s, 0, 0))
    col_doc = pl.BlockSpec((1, 1, length), lambda s, h: (s, 0, 0))
    return head, row_doc, col_doc


def attend(q, k, v, row_doc, col_doc):
    seqs, length, width = q.shape
    head, rd, cd = attention_specs(length, width)
    pairs = seqs * (width // HDIM) * length * length
    return pl.pallas_call(
        functools.partial(attend_kernel, 256),
        grid=(seqs, width // HDIM),
        in_specs=[head, head, head, rd, cd],
        out_specs=head,
        out_shape=jax.ShapeDtypeStruct(q.shape, BF16),
        compiler_params=pltpu.CompilerParams(vmem_limit_bytes=VMEM_LIMIT),
        cost_estimate=BRIEF,
        name="attend",
    )(q, k, v, row_doc, col_doc)


def attend_back(q, k, v, do, row_doc, col_doc):
    seqs, length, width = q.shape
    head, rd, cd = attention_specs(length, width)
    pairs = seqs * (width // HDIM) * length * length
    out = jax.ShapeDtypeStruct(q.shape, BF16)
    return pl.pallas_call(
        functools.partial(attend_back_kernel, 256),
        grid=(seqs, width // HDIM),
        in_specs=[head, head, head, head, rd, cd],
        out_specs=[head, head, head],
        out_shape=[out, out, out],
        scratch_shapes=[pltpu.VMEM((length, HDIM), F32), pltpu.VMEM((length, HDIM), F32)],
        compiler_params=pltpu.CompilerParams(vmem_limit_bytes=VMEM_LIMIT),
        cost_estimate=lasting(40),
        name="attend_back",
    )(q, k, v, do, row_doc, col_doc)


def project_back_kernel(
    heads, dq_ref, dk_ref, dv_ref, qp_ref, kp_ref, cos_ref, sin_ref, gq_ref, gk_ref, w_ref, dp_ref, dg_ref, *da_refs
):
    cosine, sine = cos_ref[...], -sin_ref[...]
    width = heads * HDIM

    @pl.when(pl.program_id(0) == 0)
    def _():
        dg_ref[...] = jnp.zeros_like(dg_ref)

    for n, (d_ref, pre_ref, g_ref) in enumerate(((dq_ref, qp_ref, gq_ref), (dk_ref, kp_ref, gk_ref))):
        gain = g_ref[...]
        total = jnp.zeros((1, HDIM), F32)
        for h in range(heads):
            cols = slice(h * HDIM, (h + 1) * HDIM)
            dn = turn(d_ref[:, cols].astype(F32), cosine, sine)
            pre = pre_ref[:, cols]
            scale = head_norm(pre)
            hat = pre * scale
            total += jnp.sum(dn * hat, axis=0, keepdims=True)
            inner = dn * gain
            back = scale * (inner - hat * jnp.mean(inner * hat, axis=1, keepdims=True))
            dp_ref[:, n * width + h * HDIM : n * width + (h + 1) * HDIM] = back.astype(BF16)
        dg_ref[n : n + 1, :] += total
    dp_ref[:, 2 * width :] = dv_ref[...]
    split_chunks(da_refs, slice(None), dot(dp_ref[...], w_ref[...], 1, 1))


def project_back(dq, dk, dv, q_pre, k_pre, cosine, sine, gain_q, gain_k, w, block):
    rows, width = dq.shape
    model = w.shape[0]
    form, result = chunk_form(rows // block, block, model)
    heads = width // HDIM

    def row(cols):
        return pl.BlockSpec((block, cols), lambda i: (i, 0))

    def whole(shape):
        return pl.BlockSpec(shape, lambda i: (0, 0))

    shape = jax.ShapeDtypeStruct
    return pl.pallas_call(
        functools.partial(project_back_kernel, heads),
        grid=(rows // block,),
        in_specs=[row(width)] * 5
        + [row(HDIM), row(HDIM), whole((1, HDIM)), whole((1, HDIM)), whole(w.shape)],
        out_specs=[row(3 * width), whole((8, HDIM)), *form],
        out_shape=[shape((rows, 3 * width), BF16), shape((8, HDIM), F32), *result],
        compiler_params=pltpu.CompilerParams(vmem_limit_bytes=VMEM_LIMIT),
        cost_estimate=lasting(28),
        name="project_back",
    )(dq, dk, dv, q_pre, k_pre, cosine, sine, gain_q, gain_k, w)


def join_chunks(refs, cols):
    if len(refs) == 1:
        return refs[0][:, cols]
    half = refs[0].shape[0]
    return jnp.concatenate([refs[k % 2][k // 2, 0, :, cols] for k in range(2 * half)], axis=0)


def split_chunks(refs, cols, value):
    if len(refs) == 1:
        refs[0][:, cols] = value.astype(BF16)
        return
    half, _, chunk, _ = refs[0].shape
    for k in range(2 * half):
        refs[k % 2][k // 2, 0, :, cols] = value[k * chunk : (k + 1) * chunk].astype(BF16)


def chunk_form(blocks, rows, model):
    chunk = rows // blocks
    if chunk % 16:
        return [pl.BlockSpec((rows, model), lambda i: (i, 0))], [jax.ShapeDtypeStruct((blocks * rows, model), BF16)]
    spec = pl.BlockSpec((blocks // 2, 1, chunk, model), lambda i: (0, i, 0, 0))
    return [spec] * 2, [jax.ShapeDtypeStruct((blocks // 2, blocks, chunk, model), BF16)] * 2


def by_owner(parts, blocks):
    if len(parts) == 1:
        value = parts[0]
        rows, model = value.shape[0] // blocks, value.shape[1]
        value = value.reshape(blocks, blocks // 2, 2, rows // blocks, model).transpose(2, 1, 0, 3, 4)
        parts = list(value)
    return [part.reshape(blocks // 2, -1, part.shape[-1]) for part in parts]


def expert_kernel(wide, narrow, more, parts, rank_ref, rank_col_ref, gate_ref, x_ref, dz_ref, w_ref, *refs):
    if more:
        old_out, old_dx, refs = refs[:parts], refs[parts : 2 * parts], refs[2 * parts :]
    xg_ref, dy_ref, hm_ref, dgu_ref, *refs = refs
    out_refs, dx_refs = refs[:parts], refs[parts : 2 * parts]
    dgate_ref, dzg_ref, yg_ref, dxe_ref, sum_ref = refs[2 * parts :]
    rows, model = x_ref.shape
    capacity, feed = hm_ref.shape
    hit = rank_ref[0] == lax.broadcasted_iota(jnp.int32, (capacity, rows), 0)
    sel = hit.astype(F32).astype(BF16)
    sel_back = (rank_col_ref[0] == lax.broadcasted_iota(jnp.int32, (rows, capacity), 1)).astype(F32).astype(BF16)
    gate = jnp.sum(jnp.where(hit, gate_ref[0], 0.0), axis=1, keepdims=True)

    def dispatch(i, _):
        cols = pl.ds(pl.multiple_of(i * wide, wide), wide)
        xg_ref[:, cols] = dot(sel, x_ref[:, cols], 1, 0).astype(BF16)
        dz = dot(sel, dz_ref[:, cols], 1, 0)
        dzg_ref[:, cols] = dz.astype(BF16)
        dy_ref[:, cols] = (gate * dz).astype(BF16)
        return 0

    lax.fori_loop(0, model // wide, dispatch, 0)

    def inner(i, _):
        cols = pl.ds(pl.multiple_of(i * narrow, narrow), narrow)
        ups = pl.ds(pl.multiple_of(feed + i * narrow, narrow), narrow)
        downs = pl.ds(pl.multiple_of(2 * feed + i * narrow, narrow), narrow)
        g = dot(xg_ref[...], w_ref[:, cols], 1, 0)
        u = dot(xg_ref[...], w_ref[:, ups], 1, 0)
        dh = dot(dy_ref[...], w_ref[:, downs], 1, 0)
        sig = 1.0 / (1.0 + jnp.exp(-g))
        silu = g * sig
        hm_ref[:, cols] = (silu * u).astype(BF16)
        dgu_ref[:, cols] = (dh * u * (sig + silu * (1.0 - sig))).astype(BF16)
        dgu_ref[:, ups] = (dh * silu).astype(BF16)
        return 0

    lax.fori_loop(0, feed // narrow, inner, 0)
    sum_ref[...] = jnp.zeros_like(sum_ref)

    def outer(i, _):
        cols = pl.ds(pl.multiple_of(i * narrow, narrow), narrow)
        y = dot(hm_ref[...], w_ref[cols, 2 * feed :], 1, 1).astype(BF16).astype(F32)
        part = y * dzg_ref[:, cols].astype(F32)
        total = part[:, :128]
        for j in range(1, narrow // 128):
            total += part[:, j * 128 : (j + 1) * 128]
        sum_ref[...] += total
        yg_ref[:, cols] = (gate * y).astype(BF16)
        dxe_ref[:, cols] = dot(dgu_ref[...], w_ref[cols, : 2 * feed], 1, 1).astype(BF16)
        return 0

    lax.fori_loop(0, model // narrow, outer, 0)
    dgate_ref[0] = jnp.sum(jnp.where(hit, jnp.sum(sum_ref[...], axis=1, keepdims=True), 0.0), axis=0, keepdims=True)

    def combine(i, _):
        cols = pl.ds(pl.multiple_of(i * wide, wide), wide)
        out = dot(sel_back, yg_ref[:, cols], 1, 0)
        dx = dot(sel_back, dxe_ref[:, cols], 1, 0)
        if more:
            out += join_chunks(old_out, cols).astype(F32)
            dx += join_chunks(old_dx, cols).astype(F32)
        split_chunks(out_refs, cols, out)
        split_chunks(dx_refs, cols, dx)
        return 0

    lax.fori_loop(0, model // wide, combine, 0)


def run_expert(rank, gate, x, dz, w, old, capacity, wide=2048, narrow=1024):
    blocks, rows = rank.shape
    model, feed = x.shape[1], w.shape[1] // 3
    def per_block(r, c): return pl.BlockSpec((r, c), lambda i: (i, 0))
    line = pl.BlockSpec((1, 1, rows), lambda i: (i, 0, 0))
    shape = jax.ShapeDtypeStruct
    slots = blocks * capacity
    more = bool(old)
    form, result = chunk_form(blocks, rows, model)
    xg, dy, hm, dgu, *rest = pl.pallas_call(
        functools.partial(expert_kernel, wide, narrow, more, len(form)),
        grid=(blocks,),
        in_specs=[line, pl.BlockSpec((1, rows, 1), lambda i: (i, 0, 0)), line, per_block(rows, model), per_block(rows, model),
            pl.BlockSpec(w.shape, lambda i: (0, 0), pipeline_mode=pl.Buffered(1))] + form * (2 if more else 0),
        out_specs=[per_block(capacity, model), per_block(capacity, model), per_block(capacity, feed), per_block(capacity, 2 * feed), *form, *form, line],
        out_shape=[shape((slots, model), BF16), shape((slots, model), BF16), shape((slots, feed), BF16), shape((slots, 2 * feed), BF16),
            *result, *result, shape((blocks, 1, rows), F32)],
        scratch_shapes=[pltpu.VMEM((capacity, model), BF16)] * 3 + [pltpu.VMEM((capacity, 128), F32)],
        compiler_params=pltpu.CompilerParams(vmem_limit_bytes=VMEM_LIMIT),
        cost_estimate=BRIEF,
        name="expert",
    )(rank[:, None, :], rank[:, :, None], gate[:, None, :], x, dz, w, *old)
    return xg, dy, hm, dgu, rest[: len(form)], rest[len(form) : -1], rest[-1][:, 0]


def weight_kernel(narrow, xg_ref, dy_ref, dgu_ref, hm_ref, *refs):
    *out_refs, flip_ref = refs
    base = dgu_ref.shape[1] if len(out_refs) == 1 else 0
    for src, other, out_ref, start in ((xg_ref, dgu_ref, out_refs[0], 0), (dy_ref, hm_ref, out_refs[-1], base)):
        flip_ref[...] = src[...].T
        def step(i, _):
            cols = pl.ds(pl.multiple_of(i * narrow, narrow), narrow)
            to = pl.ds(pl.multiple_of(start + i * narrow, narrow), narrow)
            out_ref[:, to] = dot(flip_ref[...], other[:, cols], 1, 0).astype(BF16)
            return 0
        lax.fori_loop(0, other.shape[1] // narrow, step, 0)


def expert_weight_grad(xg, dy, dgu, hm, parts, block=512, narrow=1024):
    slots, model = xg.shape
    feed = hm.shape[1]
    widths = (3 * feed,) if parts == 1 else (2 * feed, feed)
    cut = pl.BlockSpec((slots, block), lambda i: (0, i))
    def whole(c): return pl.BlockSpec((slots, c), lambda i: (0, 0), pipeline_mode=pl.Buffered(1))
    return pl.pallas_call(
        functools.partial(weight_kernel, narrow),
        grid=(model // block,),
        in_specs=[cut, cut, whole(2 * feed), whole(feed)],
        out_specs=[pl.BlockSpec((block, c), lambda i: (i, 0)) for c in widths],
        out_shape=[jax.ShapeDtypeStruct((model, c), BF16) for c in widths],
        scratch_shapes=[pltpu.VMEM((block, slots), BF16)],
        compiler_params=pltpu.CompilerParams(vmem_limit_bytes=VMEM_LIMIT),
        cost_estimate=BRIEF,
        name="expert_weight_grad",
    )(xg, dy, dgu, hm)

def adam_kernel(rate, w_ref, g_ref, m_ref, v_ref, *refs):
    m_out, v_out, w_out = refs[-3:]
    new = adam_step(w_ref[0], g_ref[...], m_ref[0], v_ref[0], rate)
    m_out[0], v_out[0], w_out[0] = new

def adam_expert(e, base, weight, grad, first, second, old, rate, block=128, wide=1024):
    rows, cols = grad.shape
    one = pl.BlockSpec((1, block, wide), lambda i, j: (e, i, base // wide + j))
    out = jax.ShapeDtypeStruct(weight.shape, F32)
    old = tuple(old or ())
    return pl.pallas_call(
        functools.partial(adam_kernel, rate),
        grid=(rows // block, cols // wide),
        in_specs=[one, pl.BlockSpec((block, wide), lambda i, j: (i, j)), one, one]
        + [pl.BlockSpec(memory_space=pl.ANY)] * len(old),
        out_specs=[one] * 3,
        out_shape=[out] * 3,
        input_output_aliases={4 + i: i for i in range(len(old))},
        compiler_params=pltpu.CompilerParams(vmem_limit_bytes=VMEM_LIMIT),
        cost_estimate=BRIEF,
        name="adam_expert",
    )(weight, grad, first, second, *old)


def norm_back(dn, value, gain):
    scale = lax.rsqrt(jnp.mean(value * value, axis=-1, keepdims=True) + NORM_EPS)
    hat = value * scale
    inner = dn * gain
    back = scale * (inner - hat * jnp.mean(inner * hat, axis=-1, keepdims=True))
    return back, jnp.sum(dn * hat, axis=0)


def after(value, *others):
    return lax.optimization_barrier((value, *others))[0]


def body(
    tokens,
    cotangent,
    doc_lengths,
    routes,
    attn_weight,
    router_weight,
    gain_values,
    expert_weight,
    attn_first,
    attn_second,
    router_first,
    router_second,
    gain_first,
    gain_second,
    expert_first,
    expert_second,
):
    fsdp_count, seq_count = lax.axis_size("fsdp"), lax.axis_size("seq")
    everywhere = ("seq", "fsdp")
    here, plane = lax.axis_index("fsdp"), lax.axis_index("seq")
    around = here ^ jnp.arange(fsdp_count, dtype=jnp.int32)
    planes = plane ^ jnp.arange(seq_count, dtype=jnp.int32)
    rows, model = tokens.shape[1:]
    length = rows * seq_count
    experts = EXP_DEV * fsdp_count
    capacity = (rows * TOP // experts * 4 // 3 + 7) // 8 * 8
    width = model // fsdp_count
    shard = attn_weight.shape[0]
    members, chunk = fsdp_count // seq_count, rows // fsdp_count
    blocks = fsdp_count

    def blocked(parts):
        stacked = jnp.stack([part.reshape(blocks, chunk, -1) for part in parts], axis=1)
        return stacked.reshape(blocks * rows, -1)

    def pieces(value):
        cut = value.reshape(blocks, fsdp_count, chunk, -1)
        return [cut[:, k].reshape(rows, -1) for k in range(fsdp_count)]

    with jax.named_scope("gather_wo"):
        out_part = gather_direct(attn_weight[:, 3 * model :], "seq", seq_count)
    with jax.named_scope("remap_x"):
        x_low = to_plane_seq(to_plane_fsdp(tokens[0], fsdp_count), seq_count, fsdp_count)
    with jax.named_scope("gather_wqkv"):
        first_part = attn_weight[:, : 3 * model].reshape(shard, 3, fsdp_count, width).transpose(2, 0, 1, 3)
        first_part = reorder(first_part.reshape(fsdp_count, shard, 3 * width), around)
        first_part = reorder(jnp.stack(exchange(list(first_part), "fsdp", fsdp_count)), around)
        in_proj = lax.all_gather(first_part.reshape(fsdp_count * shard, 3 * width), "seq", axis=0, tiled=True)
    with jax.named_scope("gather_small"):
        flat = [router_weight.reshape(-1), gain_values, routes.reshape(-1), doc_lengths.reshape(-1)]
        sizes = [v.shape[0] for v in flat]
        starts = [sum(sizes[:i]) for i in range(len(sizes))]
        flat = after(jnp.concatenate([v.astype(F32) for v in flat]), x_low)
        flat = jnp.pad(flat, (0, -flat.shape[0] % 1024)).reshape(-1, 128)
        lines = flat.shape[0]
        small_all = lax.all_gather(flat, "seq", axis=0, tiled=True)
        small_all = lax.all_gather(small_all, "fsdp", axis=0, tiled=True)
        every = small_all.reshape(fsdp_count, seq_count, lines * 128)
        per_device = every.transpose(1, 0, 2).reshape(seq_count * fsdp_count, lines * 128)
        full_router = per_device[:, : sizes[0]].reshape(model, experts).astype(BF16)
        gains = per_device[:, starts[1] : starts[2]].reshape(-1)
        attn_gain, ffn_gain = gains[:model], gains[model : 2 * model]
        gain_q = gains[2 * model : 2 * model + HDIM][None]
        gain_k = gains[2 * model + HDIM : 2 * model + 2 * HDIM][None]
        meta = lax.dynamic_slice_in_dim(every, plane * members, members, 0)[:, :, starts[2] : starts[3] + 3]
        meta = meta.astype(jnp.int32)
    docs = meta[:, 0, rows * TOP : rows * TOP + 3]
    routes_all = meta[:, :, : rows * TOP].reshape(blocks, fsdp_count, chunk, TOP)
    routes_all = reorder(routes_all, around, 1).reshape(blocks, rows, TOP)
    positions = (
        jnp.arange(seq_count, dtype=jnp.int32)[:, None, None] * rows
        + around[None, :, None] * chunk
        + jnp.arange(chunk, dtype=jnp.int32)[None, None, :]
    ).reshape(1, length)
    doc_index = (positions >= docs[:, :1]).astype(jnp.int32) + (
        positions >= docs[:, :1] + docs[:, 1:2]
    ).astype(jnp.int32)
    row_doc, col_doc = doc_index[:, :, None], doc_index[:, None, :]
    frequency = ROPE_BASE ** (-jnp.arange(HDIM // 2, dtype=F32) / (HDIM // 2))
    angles = positions[0].astype(F32)[:, None] * frequency[None, :]
    cosine, sine = jnp.cos(angles), jnp.sin(angles)
    cosine = jnp.concatenate([cosine, cosine], axis=1)
    sine = jnp.concatenate([-sine, sine], axis=1)

    with jax.named_scope("gather_experts"):
        expert_later = after(expert_weight, first_part)
        expert_full = [lax.all_gather(expert_later[e], "seq", axis=0, tiled=True) for e in range(EXP_DEV)]
    with jax.named_scope("gather_wo"):
        out_part = jnp.stack(plane_gather(fsdp_count, out_part.reshape(seq_count * shard, model)))
        out_part = out_part.reshape(fsdp_count * seq_count, shard, model)
        place = jnp.arange(seq_count * fsdp_count, dtype=jnp.int32)
        place = (here ^ (place % fsdp_count)) * seq_count + (plane ^ (place // fsdp_count))
        out_proj = reorder(out_part, place).reshape(model, model)
    with jax.named_scope("gather_x"):
        x_all = blocked(plane_gather(fsdp_count, x_low))
    with jax.named_scope("remap_dz"):
        dz_low = to_plane_seq(to_plane_fsdp(after(cotangent[0], x_all), fsdp_count), seq_count, fsdp_count)

    own = here * EXP_DEV + jnp.arange(EXP_DEV, dtype=jnp.int32)
    named = jnp.any(routes_all[:, None, :, :] == own[None, :, None, None], axis=3)
    before = jnp.cumsum(named.astype(jnp.int32), axis=2) - named.astype(jnp.int32)
    rank = jnp.where(named, before, -1)
    chosen = jnp.any(
        routes_all[:, :, :, None] == jnp.arange(experts, dtype=jnp.int32)[None, None, None, :], axis=2
    )

    cosine_all, sine_all = jnp.tile(cosine, (members, 1)), jnp.tile(sine, (members, 1))
    a_all, q_low, k_low, v_low, q_pre, k_pre = project(
        x_all, attn_gain[None], in_proj, cosine_all, sine_all, gain_q, gain_k, rows
    )
    with jax.named_scope("gather_dz"):
        dz_all = blocked(plane_gather(fsdp_count, dz_low))
    seq_shape = (members, length, width)
    q_seq, k_seq, v_seq = (t.reshape(seq_shape) for t in (q_low, k_low, v_low))
    o_all = attend(q_seq, k_seq, v_seq, row_doc, col_doc)
    with jax.named_scope("o_exchange"):
        o_own = reorder(o_all.reshape(blocks, fsdp_count, chunk, width), around, 1)
        o_own = o_own.transpose(1, 0, 2, 3).reshape(fsdp_count, rows, width)
        o_own = lax.all_to_all(o_own, "fsdp", split_axis=0, concat_axis=0, tiled=True)
        o_own = o_own.transpose(1, 0, 2).reshape(rows, model)
    inputs = x_low.astype(F32)
    middle = inputs + dot(o_own, out_proj, 1, 0)
    middle_scale = lax.rsqrt(jnp.mean(middle * middle, axis=-1, keepdims=True) + NORM_EPS)
    normed = (middle * middle_scale * ffn_gain).astype(BF16)

    with jax.named_scope("gather_xn"):
        xn_all = blocked(plane_gather(fsdp_count, normed))
    with jax.named_scope("gates"):
        logits = dot(xn_all, full_router, 1, 0).reshape(blocks, rows, experts)
        top = jnp.max(jnp.where(chosen, logits, -jnp.inf), axis=2, keepdims=True)
        raised = jnp.where(chosen, jnp.exp(logits - top), 0.0)
        gates = raised / jnp.sum(raised, axis=2, keepdims=True)
        gates_mine = lax.dynamic_slice_in_dim(gates, here * EXP_DEV, EXP_DEV, axis=2)
    sums, gate_back, expert_share, held = (), [], [], None
    for e in range(EXP_DEV):
        with jax.named_scope(f"expert{e}"):
            w = expert_full[e] if held is None else after(expert_full[e], *held)
            xg, dy, hm, dgu, mixed, dxn, dgate = run_expert(
                rank[:, e], gates_mine[:, :, e], xn_all, dz_all, w, sums, capacity
            )
            sums = (*mixed, *dxn)
            gate_back.append(dgate)
            if e == EXP_DEV - 1:
                gate_parts = exchange(pieces(jnp.stack(gate_back, axis=2)), "fsdp", fsdp_count)
                dxn = Scatter(fsdp_count, *by_owner(dxn, blocks), hold=gate_parts)
                xg = after(xg, *dxn.sends)
            held = expert_weight_grad(xg, dy, dgu, hm, 1 if e < EXP_DEV - 1 else 2)
            if e < EXP_DEV - 1:
                expert_share.append(lax.psum_scatter(held[0], "seq", scatter_dimension=0, tiled=True))
    last_up = lax.psum_scatter(held[0], "seq", scatter_dimension=0, tiled=True)

    with jax.named_scope("router_back"):
        gate_grad = reorder(jnp.stack(gate_parts, axis=1), around, 1).reshape(rows, experts)
        gates_own, chosen_own = pieces(gates)[0], pieces(chosen)[0]
        gate_grad = jnp.where(chosen_own, gate_grad, 0.0)
        dlog = (gates_own * (gate_grad - jnp.sum(gates_own * gate_grad, axis=1, keepdims=True))).astype(BF16)
    with jax.named_scope("scatter_dxn"):
        dxn_own = dxn.second(*held).third()
    dxn_own = dxn_own + dot(dlog, full_router, 1, 1)
    middle_back, ffn_gain_grad = norm_back(dxn_own, middle, ffn_gain)
    middle_grad = dz_low.astype(F32) + middle_back
    db = middle_grad.astype(BF16)

    with jax.named_scope("do_exchange"):
        do_own = dot(db, out_proj, 1, 1).astype(BF16).reshape(rows, fsdp_count, width).transpose(1, 0, 2)
        do_own = lax.all_to_all(do_own, "fsdp", split_axis=0, concat_axis=0, tiled=True)
        do_all = reorder(do_own, around).reshape(fsdp_count, blocks, chunk, width).transpose(1, 0, 2, 3)
        do_all = do_all.reshape(seq_shape)
    with jax.named_scope("scatter_out"):
        near, far = by_owner(mixed, blocks)
        mixed = Scatter(fsdp_count, near, after(far, db), hold=(do_all,))
    do_all = after(do_all, expert_share[0], *mixed.sends)
    dq, dk, dv = (
        t.reshape(-1, width) for t in attend_back(q_seq, k_seq, v_seq, do_all, row_doc, col_doc)
    )
    with jax.named_scope("scatter_out"):
        mixed = mixed.second(dq)
    d_proj, gain_qk, *da_part = project_back(
        after(dq, *mixed.lasts), dk, dv, q_pre, k_pre, cosine_all, sine_all, gain_q, gain_k, in_proj, rows
    )
    with jax.named_scope("scatter_out"):
        layer_low = (middle + mixed.third(d_proj)).astype(BF16)
    with jax.named_scope("scatter_da"):
        near, far = by_owner(da_part, blocks)
        da = Scatter(fsdp_count, near, after(far, layer_low))
    with jax.named_scope("remap_out"):
        layer_out = from_plane_seq(layer_low, seq_count, fsdp_count)
    with jax.named_scope("weight_grads"):
        in_grad = dot(after(a_all, *da.sends), d_proj, 0, 0).astype(BF16)
        in_share = lax.psum_scatter(in_grad, "seq", scatter_dimension=0, tiled=True)
        moments = (expert_first, expert_second)
        expert_new = None
        for e in range(EXP_DEV - 1):
            share = after(expert_share[e], *da.sends)
            expert_new = adam_expert(e, 0, expert_weight, share, *moments, expert_new, RATE_EXPERT)
    with jax.named_scope("scatter_da"):
        da = da.second(in_grad, expert_new[0])
    last_down = lax.psum_scatter(after(held[1], *da.lasts), "seq", scatter_dimension=0, tiled=True)
    with jax.named_scope("weight_grads"):
        out_grad = dot(after(o_own, *da.lasts), db, 0, 0).astype(BF16)
        out_grad = out_grad.reshape(seq_count, fsdp_count, shard, model)
        pairs = reorder(around, jnp.arange(fsdp_count).reshape(-1, 2).T.reshape(-1))
        out_grad = reorder(out_grad, pairs, 1).transpose(1, 0, 2, 3)
        out_grad = out_grad.reshape(2, fsdp_count // 2, seq_count * shard, model)
    with jax.named_scope("scatter_da"):
        da_own = da.third(out_grad, layer_out)
    input_back, attn_gain_grad = norm_back(da_own, inputs, attn_gain)
    input_low = (middle_grad + input_back).astype(BF16)
    with jax.named_scope("remap_grad"):
        input_grad = from_plane_seq(input_low, seq_count, fsdp_count)
    with jax.named_scope("small_sum"):
        router_grad = dot(normed, dlog, 0, 0)
        small = jnp.concatenate(
            [router_grad.reshape(-1), attn_gain_grad, ffn_gain_grad, gain_qk[0], gain_qk[1]]
        )
        small = plane_sum(small, fsdp_count)
        own_router, own_gain = shard * experts, gain_values.shape[0]

        def own_part(p):
            device = p * fsdp_count + here
            return jnp.concatenate(
                [
                    lax.dynamic_slice_in_dim(small, device * own_router, own_router),
                    lax.dynamic_slice_in_dim(small, model * experts + device * own_gain, own_gain),
                ]
            )

        small_parts = [own_part(planes[m]) for m in range(seq_count)]
    with jax.named_scope("scatter_wo"):
        out_grad = Scatter(fsdp_count, out_grad[0], after(out_grad[1], input_low), hold=small_parts)
    last = EXP_DEV - 1
    expert_new = adam_expert(
        last, 0, expert_weight, after(last_up, *out_grad.sends), *moments, expert_new, RATE_EXPERT
    )
    with jax.named_scope("scatter_wo"):
        out_grad = out_grad.second(expert_new[0])
        out_share = out_grad.third().astype(BF16)
    with jax.named_scope("scatter_wo"):
        out_sent = reorder(out_share.reshape(seq_count, shard, model), planes)
        out_parts = exchange(list(out_sent), "seq", seq_count)
    with jax.named_scope("scatter_wqkv"):
        in_share = after(in_share, out_sent)
        in_share = sent = reorder(in_share.reshape(fsdp_count, shard, 3 * width), around)
        in_share = reorder(jnp.stack(exchange(list(in_share), "fsdp", fsdp_count)), around)
        in_share = in_share.reshape(fsdp_count, shard, 3, width).transpose(1, 2, 0, 3).reshape(shard, 3 * model)
    with jax.named_scope("remap"):
        both = jnp.concatenate([input_grad, layer_out], axis=1)
        both = from_plane_fsdp(after(both, sent), fsdp_count)
        input_grad, layer_out = both[:, :model].astype(F32), both[:, model:]
    out_share = sum(p.astype(F32) for p in out_parts)
    small_own = sum(exchange(list(lax.optimization_barrier((*small_parts, in_share))[:-1]), "seq", seq_count))
    router_share, gain_share = small_own[:own_router].reshape(shard, experts), small_own[own_router:]

    attn_share = jnp.concatenate([in_share.astype(F32), out_share], axis=1)
    attn_new = adam_step(attn_weight, attn_share, attn_first, attn_second, RATE_ATTN)
    router_new = adam_step(router_weight, router_share, router_first, router_second, RATE_ROUTER)
    expert_new = adam_expert(
        last, 2 * FFE, expert_weight, after(last_down, attn_new[0]), *moments, expert_new, RATE_EXPERT
    )
    gain_new = adam_step(gain_values, gain_share, gain_first, gain_second, RATE_GAIN)
    return (layer_out[None], input_grad[None], *attn_new, *router_new, *gain_new, *expert_new)


def solution(mesh):
    tokens = P("fsdp", "seq", None)
    matrix, vector = P(("seq", "fsdp"), None), P(("seq", "fsdp"))
    return jax.shard_map(
        body,
        mesh=mesh,
        in_specs=(
            tokens,
            tokens,
            P("fsdp", None),
            tokens,
            matrix,
            matrix,
            vector,
            tokens,
            matrix,
            matrix,
            matrix,
            matrix,
            vector,
            vector,
            tokens,
            tokens,
        ),
        out_specs=(
            tokens,
            tokens,
            matrix,
            matrix,
            matrix,
            matrix,
            matrix,
            matrix,
            vector,
            vector,
            vector,
            tokens,
            tokens,
            tokens,
        ),
        check_vma=False,
    )
```

```python
import functools
import math

import jax
import jax.numpy as jnp
from jax import lax
from jax.experimental import pallas as pl
from jax.experimental.pallas import tpu as pltpu
from jax.sharding import PartitionSpec as P

HEADS = 16
HDIM = 128
FFE = 1024
TOP = 8
EXP_DEV = 2
STEP = 10

NORM_EPS = 1e-06
ROPE_BASE = 10000.0
BETA_ONE = 0.9
BETA_TWO = 0.95
ADAM_EPS = 1e-08
WEIGHT_DECAY = 0.1
RATE_ATTN = 0.1
RATE_ROUTER = 0.03
RATE_GAIN = 0.5
RATE_EXPERT = 0.1
VMEM_LIMIT = 56 * 1024 * 1024

BRIEF = pl.CostEstimate(flops=1000, bytes_accessed=1000, transcendentals=0)


def lasting(us):
    return pl.CostEstimate(flops=int(us * 1e9), bytes_accessed=1000, transcendentals=0)


F32 = jnp.float32
BF16 = jnp.bfloat16


def dot(a, b, ca, cb):
    return lax.dot_general(a, b, (((ca,), (cb,)), ((), ())), preferred_element_type=F32)


def adam_step(weight, gradient, first_state, second, step_rate):
    gradient = gradient.astype(F32)
    first_new = BETA_ONE * first_state + (1.0 - BETA_ONE) * gradient
    second_new = BETA_TWO * second + (1.0 - BETA_TWO) * gradient * gradient
    first_hat = first_new / (1.0 - BETA_ONE**STEP)
    second_hat = second_new / (1.0 - BETA_TWO**STEP)
    master = weight.astype(F32) * (1.0 - step_rate * WEIGHT_DECAY) - step_rate * first_hat / (
        jnp.sqrt(second_hat) + ADAM_EPS
    )
    return first_new, second_new, master


def swap(value, step, axis, count):
    return lax.ppermute(value, axis, [(i, i ^ step) for i in range(count)])


def gather_direct(value, axis, count):
    return jnp.stack([value] + [swap(value, k, axis, count) for k in range(1, count)])


def exchange(parts, axis, count):
    return [parts[0]] + [swap(parts[k], k, axis, count) for k in range(1, count)]


def reorder(stacked, index, axis=0):
    return jnp.take(stacked, index, axis=axis, mode="clip")


def plane_gather(count, value):
    if count != 8:
        whole = lax.all_gather(value, "fsdp")
        mine = lax.axis_index("fsdp")
        return [lax.dynamic_index_in_dim(whole, mine ^ k, 0, False) for k in range(count)]
    go = functools.partial(swap, axis="fsdp", count=count)
    half = value.shape[0] // 2
    by_x, by_y = go(value, 2), go(value, 4)
    far = jnp.concatenate([go(by_x[:half], 4), go(by_y[half:], 2)], axis=0)
    return [value, go(value, 1), by_x, go(by_x, 1), by_y, go(by_y, 1), far, go(far, 1)]


class Scatter:
    def __init__(self, count, near, far, hold=()):
        self.count, self.near = count, near
        if count != 8:
            stacked = jnp.stack([near, far], axis=1).reshape(count, *near.shape[1:])
            stacked = reorder(stacked, lax.axis_index("fsdp") ^ jnp.arange(count))
            self.sum = lax.psum_scatter(stacked, "fsdp", scatter_dimension=0).astype(F32)
            self.got, self.sends, self.lasts = self.sum, (self.sum,), (self.sum,)
            return
        self.half = near.shape[1] // 2
        self.got = swap(far, 1, "fsdp", count)
        sends = (self.total(slice(1, None, 2), 0).astype(BF16), self.total(slice(2, None), 1).astype(BF16))
        if hold:
            sends = lax.optimization_barrier((*sends, *hold))[:2]
        self.sends = sends

    def total(self, index, part):
        rows = slice(self.half * part, self.half * (part + 1))
        return self.near[index, rows].astype(F32) + self.got[index, rows].astype(F32)

    def second(self, *beside):
        if self.count == 8:
            self.by_x = swap(self.sends[0], 2, "fsdp", self.count)
            self.by_y = swap(self.sends[1], 4, "fsdp", self.count)
            if beside:
                self.by_x, self.by_y = lax.optimization_barrier((self.by_x, self.by_y, *beside))[:2]
            self.lasts = (
                (self.total(2, 0) + self.by_x[1].astype(F32)).astype(BF16),
                (self.total(1, 1) + self.by_y[1].astype(F32)).astype(BF16),
            )
        return self

    def third(self, *beside):
        if self.count != 8:
            return self.sum
        y_last = swap(self.lasts[0], 4, "fsdp", self.count)
        x_last = swap(self.lasts[1], 2, "fsdp", self.count)
        if beside:
            y_last, x_last = lax.optimization_barrier((y_last, x_last, *beside))[:2]
        top = self.total(0, 0) + self.by_x[0].astype(F32) + y_last.astype(F32)
        low = self.total(0, 1) + self.by_y[0].astype(F32) + x_last.astype(F32)
        return jnp.concatenate([top, low], axis=0)


def plane_sum(value, fsdp_count):
    step = 1
    while step < fsdp_count:
        value = value + swap(value, step, "fsdp", fsdp_count)
        step *= 2
    return value


def to_plane_fsdp(value, fsdp_count):
    value = value.reshape(fsdp_count, -1, value.shape[1])
    return lax.all_to_all(value, "fsdp", split_axis=0, concat_axis=0, tiled=True)


def to_plane_seq(value, seq_count, fsdp_count):
    _, chunk, width = value.shape
    members = fsdp_count // seq_count
    value = value.reshape(seq_count, members * chunk, width)
    value = lax.all_to_all(value, "seq", split_axis=0, concat_axis=0, tiled=True)
    value = value.reshape(seq_count, members, chunk, width).transpose(1, 0, 2, 3)
    return value.reshape(fsdp_count * chunk, width)


def from_plane_seq(value, seq_count, fsdp_count):
    rows, width = value.shape
    members, chunk = fsdp_count // seq_count, rows // fsdp_count
    value = value.reshape(members, seq_count, chunk, width).transpose(1, 0, 2, 3)
    value = value.reshape(seq_count, members * chunk, width)
    return lax.all_to_all(value, "seq", split_axis=0, concat_axis=0, tiled=True).reshape(rows, width)


def from_plane_fsdp(value, fsdp_count):
    rows, width = value.shape
    value = value.reshape(fsdp_count, rows // fsdp_count, width)
    return lax.all_to_all(value, "fsdp", split_axis=0, concat_axis=0, tiled=True).reshape(rows, width)


def head_norm(value):
    return lax.rsqrt(jnp.mean(value * value, axis=-1, keepdims=True) + NORM_EPS)


def turn(value, cosine, sine):
    return value * cosine + pltpu.roll(value, HDIM // 2, 1) * sine


def project_kernel(
    heads, x_ref, gain_ref, w_ref, cos_ref, sin_ref, gq_ref, gk_ref, a_ref, q_ref, k_ref, v_ref, qp_ref, kp_ref
):
    x = x_ref[...].astype(F32)
    a = (x * head_norm(x) * gain_ref[...]).astype(BF16)
    a_ref[...] = a
    width = heads * HDIM
    cosine, sine = cos_ref[...], sin_ref[...]
    for n, (low_ref, pre_ref, g_ref) in enumerate(((q_ref, qp_ref, gq_ref), (k_ref, kp_ref, gk_ref))):
        part = dot(a, w_ref[:, n * width : (n + 1) * width], 1, 0)
        pre_ref[...] = part
        for h in range(heads):
            cols = slice(h * HDIM, (h + 1) * HDIM)
            one = part[:, cols]
            low_ref[:, cols] = turn(one * head_norm(one) * g_ref[...], cosine, sine).astype(BF16)
    v_ref[...] = dot(a, w_ref[:, 2 * width :], 1, 0).astype(BF16)


def project(x, gain, w, cosine, sine, gain_q, gain_k, block):
    rows, model = x.shape
    width = w.shape[1] // 3
    heads = width // HDIM

    def row(cols):
        return pl.BlockSpec((block, cols), lambda i: (i, 0))

    def whole(shape):
        return pl.BlockSpec(shape, lambda i: (0, 0))

    shape = jax.ShapeDtypeStruct
    return pl.pallas_call(
        functools.partial(project_kernel, heads),
        grid=(rows // block,),
        in_specs=[
            row(model),
            whole((1, model)),
            whole(w.shape),
            row(HDIM),
            row(HDIM),
            whole((1, HDIM)),
            whole((1, HDIM)),
        ],
        out_specs=[row(model), row(width), row(width), row(width), row(width), row(width)],
        out_shape=[
            shape((rows, model), BF16),
            shape((rows, width), BF16),
            shape((rows, width), BF16),
            shape((rows, width), BF16),
            shape((rows, width), F32),
            shape((rows, width), F32),
        ],
        compiler_params=pltpu.CompilerParams(vmem_limit_bytes=VMEM_LIMIT),
        cost_estimate=BRIEF,
        name="project",
    )(x, gain, w, cosine, sine, gain_q, gain_k)


SCORE = HDIM**-0.5


def probabilities(q, k, row_doc, col_doc):
    scores = dot(q, k, 1, 1) * (SCORE * math.log2(math.e))
    weight = jnp.where(row_doc == col_doc, jnp.exp2(scores), 0.0)
    return weight * (1.0 / jnp.sum(weight, axis=1, keepdims=True))


def attend_kernel(block, q_ref, k_ref, v_ref, rd_ref, cd_ref, o_ref):
    k, v = k_ref[0], v_ref[0]

    def step(i, _):
        rows = pl.ds(i * block, block)
        p = probabilities(q_ref[0, rows, :], k, rd_ref[0, rows, :], cd_ref[0])
        o_ref[0, rows, :] = dot(p.astype(BF16), v, 1, 0).astype(BF16)
        return 0

    lax.fori_loop(0, q_ref.shape[1] // block, step, 0)


def attend_back_kernel(block, q_ref, k_ref, v_ref, do_ref, rd_ref, cd_ref, dq_ref, dk_ref, dv_ref, sk_ref, sv_ref):
    k, v = k_ref[0], v_ref[0]
    sk_ref[...] = jnp.zeros_like(sk_ref)
    sv_ref[...] = jnp.zeros_like(sv_ref)

    def step(i, _):
        rows = pl.ds(i * block, block)
        q, do = q_ref[0, rows, :], do_ref[0, rows, :]
        p = probabilities(q, k, rd_ref[0, rows, :], cd_ref[0])
        dp = dot(do, v, 1, 1)
        ds = (p * (dp - jnp.sum(p * dp, axis=1, keepdims=True))).astype(BF16)
        dq_ref[0, rows, :] = (dot(ds, k, 1, 0) * SCORE).astype(BF16)
        sk_ref[...] += dot(ds, q, 0, 0)
        sv_ref[...] += dot(p.astype(BF16), do, 0, 0)
        return 0

    lax.fori_loop(0, q_ref.shape[1] // block, step, 0)
    dk_ref[0] = (sk_ref[...] * SCORE).astype(BF16)
    dv_ref[0] = sv_ref[...].astype(BF16)


def attention_specs(length, width):
    head = pl.BlockSpec((1, length, HDIM), lambda s, h: (s, 0, h))
    row_doc = pl.BlockSpec((1, length, 1), lambda s, h: (s, 0, 0))
    col_doc = pl.BlockSpec((1, 1, length), lambda s, h: (s, 0, 0))
    return head, row_doc, col_doc


def attend(q, k, v, row_doc, col_doc):
    seqs, length, width = q.shape
    head, rd, cd = attention_specs(length, width)
    pairs = seqs * (width // HDIM) * length * length
    return pl.pallas_call(
        functools.partial(attend_kernel, 256),
        grid=(seqs, width // HDIM),
        in_specs=[head, head, head, rd, cd],
        out_specs=head,
        out_shape=jax.ShapeDtypeStruct(q.shape, BF16),
        compiler_params=pltpu.CompilerParams(vmem_limit_bytes=VMEM_LIMIT),
        cost_estimate=BRIEF,
        name="attend",
    )(q, k, v, row_doc, col_doc)


def attend_back(q, k, v, do, row_doc, col_doc):
    seqs, length, width = q.shape
    head, rd, cd = attention_specs(length, width)
    pairs = seqs * (width // HDIM) * length * length
    out = jax.ShapeDtypeStruct(q.shape, BF16)
    return pl.pallas_call(
        functools.partial(attend_back_kernel, 256),
        grid=(seqs, width // HDIM),
        in_specs=[head, head, head, head, rd, cd],
        out_specs=[head, head, head],
        out_shape=[out, out, out],
        scratch_shapes=[pltpu.VMEM((length, HDIM), F32), pltpu.VMEM((length, HDIM), F32)],
        compiler_params=pltpu.CompilerParams(vmem_limit_bytes=VMEM_LIMIT),
        cost_estimate=lasting(40),
        name="attend_back",
    )(q, k, v, do, row_doc, col_doc)


def project_back_kernel(
    heads, dq_ref, dk_ref, dv_ref, qp_ref, kp_ref, cos_ref, sin_ref, gq_ref, gk_ref, w_ref, dp_ref, dg_ref, *da_refs
):
    cosine, sine = cos_ref[...], -sin_ref[...]
    width = heads * HDIM

    @pl.when(pl.program_id(0) == 0)
    def _():
        dg_ref[...] = jnp.zeros_like(dg_ref)

    for n, (d_ref, pre_ref, g_ref) in enumerate(((dq_ref, qp_ref, gq_ref), (dk_ref, kp_ref, gk_ref))):
        gain = g_ref[...]
        total = jnp.zeros((1, HDIM), F32)
        for h in range(heads):
            cols = slice(h * HDIM, (h + 1) * HDIM)
            dn = turn(d_ref[:, cols].astype(F32), cosine, sine)
            pre = pre_ref[:, cols]
            scale = head_norm(pre)
            hat = pre * scale
            total += jnp.sum(dn * hat, axis=0, keepdims=True)
            inner = dn * gain
            back = scale * (inner - hat * jnp.mean(inner * hat, axis=1, keepdims=True))
            dp_ref[:, n * width + h * HDIM : n * width + (h + 1) * HDIM] = back.astype(BF16)
        dg_ref[n : n + 1, :] += total
    dp_ref[:, 2 * width :] = dv_ref[...]
    split_chunks(da_refs, slice(None), dot(dp_ref[...], w_ref[...], 1, 1))


def project_back(dq, dk, dv, q_pre, k_pre, cosine, sine, gain_q, gain_k, w, block):
    rows, width = dq.shape
    model = w.shape[0]
    form, result = chunk_form(rows // block, block, model)
    heads = width // HDIM

    def row(cols):
        return pl.BlockSpec((block, cols), lambda i: (i, 0))

    def whole(shape):
        return pl.BlockSpec(shape, lambda i: (0, 0))

    shape = jax.ShapeDtypeStruct
    return pl.pallas_call(
        functools.partial(project_back_kernel, heads),
        grid=(rows // block,),
        in_specs=[row(width)] * 5
        + [row(HDIM), row(HDIM), whole((1, HDIM)), whole((1, HDIM)), whole(w.shape)],
        out_specs=[row(3 * width), whole((8, HDIM)), *form],
        out_shape=[shape((rows, 3 * width), BF16), shape((8, HDIM), F32), *result],
        compiler_params=pltpu.CompilerParams(vmem_limit_bytes=VMEM_LIMIT),
        cost_estimate=lasting(28),
        name="project_back",
    )(dq, dk, dv, q_pre, k_pre, cosine, sine, gain_q, gain_k, w)


def join_chunks(refs, cols):
    if len(refs) == 1:
        return refs[0][:, cols]
    half = refs[0].shape[0]
    return jnp.concatenate([refs[k % 2][k // 2, 0, :, cols] for k in range(2 * half)], axis=0)


def split_chunks(refs, cols, value):
    if len(refs) == 1:
        refs[0][:, cols] = value.astype(BF16)
        return
    half, _, chunk, _ = refs[0].shape
    for k in range(2 * half):
        refs[k % 2][k // 2, 0, :, cols] = value[k * chunk : (k + 1) * chunk].astype(BF16)


def chunk_form(blocks, rows, model):
    chunk = rows // blocks
    if chunk % 16:
        return [pl.BlockSpec((rows, model), lambda i: (i, 0))], [jax.ShapeDtypeStruct((blocks * rows, model), BF16)]
    spec = pl.BlockSpec((blocks // 2, 1, chunk, model), lambda i: (0, i, 0, 0))
    return [spec] * 2, [jax.ShapeDtypeStruct((blocks // 2, blocks, chunk, model), BF16)] * 2


def by_owner(parts, blocks):
    if len(parts) == 1:
        value = parts[0]
        rows, model = value.shape[0] // blocks, value.shape[1]
        value = value.reshape(blocks, blocks // 2, 2, rows // blocks, model).transpose(2, 1, 0, 3, 4)
        parts = list(value)
    return [part.reshape(blocks // 2, -1, part.shape[-1]) for part in parts]


def expert_kernel(wide, narrow, more, parts, rank_ref, rank_col_ref, gate_ref, x_ref, dz_ref, w_ref, *refs):
    if more:
        old_out, old_dx, refs = refs[:parts], refs[parts : 2 * parts], refs[2 * parts :]
    xg_ref, dy_ref, hm_ref, dgu_ref, *refs = refs
    out_refs, dx_refs = refs[:parts], refs[parts : 2 * parts]
    dgate_ref, dzg_ref, yg_ref, dxe_ref, sum_ref = refs[2 * parts :]
    rows, model = x_ref.shape
    capacity, feed = hm_ref.shape
    hit = rank_ref[0] == lax.broadcasted_iota(jnp.int32, (capacity, rows), 0)
    sel = hit.astype(F32).astype(BF16)
    sel_back = (rank_col_ref[0] == lax.broadcasted_iota(jnp.int32, (rows, capacity), 1)).astype(F32).astype(BF16)
    gate = jnp.sum(jnp.where(hit, gate_ref[0], 0.0), axis=1, keepdims=True)

    def dispatch(i, _):
        cols = pl.ds(pl.multiple_of(i * wide, wide), wide)
        xg_ref[:, cols] = dot(sel, x_ref[:, cols], 1, 0).astype(BF16)
        dz = dot(sel, dz_ref[:, cols], 1, 0)
        dzg_ref[:, cols] = dz.astype(BF16)
        dy_ref[:, cols] = (gate * dz).astype(BF16)
        return 0

    lax.fori_loop(0, model // wide, dispatch, 0)

    def inner(i, _):
        cols = pl.ds(pl.multiple_of(i * narrow, narrow), narrow)
        ups = pl.ds(pl.multiple_of(feed + i * narrow, narrow), narrow)
        downs = pl.ds(pl.multiple_of(2 * feed + i * narrow, narrow), narrow)
        g = dot(xg_ref[...], w_ref[:, cols], 1, 0)
        u = dot(xg_ref[...], w_ref[:, ups], 1, 0)
        dh = dot(dy_ref[...], w_ref[:, downs], 1, 0)
        sig = 1.0 / (1.0 + jnp.exp(-g))
        silu = g * sig
        hm_ref[:, cols] = (silu * u).astype(BF16)
        dgu_ref[:, cols] = (dh * u * (sig + silu * (1.0 - sig))).astype(BF16)
        dgu_ref[:, ups] = (dh * silu).astype(BF16)
        return 0

    lax.fori_loop(0, feed // narrow, inner, 0)
    sum_ref[...] = jnp.zeros_like(sum_ref)

    def outer(i, _):
        cols = pl.ds(pl.multiple_of(i * narrow, narrow), narrow)
        y = dot(hm_ref[...], w_ref[cols, 2 * feed :], 1, 1).astype(BF16).astype(F32)
        part = y * dzg_ref[:, cols].astype(F32)
        total = part[:, :128]
        for j in range(1, narrow // 128):
            total += part[:, j * 128 : (j + 1) * 128]
        sum_ref[...] += total
        yg_ref[:, cols] = (gate * y).astype(BF16)
        dxe_ref[:, cols] = dot(dgu_ref[...], w_ref[cols, : 2 * feed], 1, 1).astype(BF16)
        return 0

    lax.fori_loop(0, model // narrow, outer, 0)
    dgate_ref[0] = jnp.sum(jnp.where(hit, jnp.sum(sum_ref[...], axis=1, keepdims=True), 0.0), axis=0, keepdims=True)

    def combine(i, _):
        cols = pl.ds(pl.multiple_of(i * wide, wide), wide)
        out = dot(sel_back, yg_ref[:, cols], 1, 0)
        dx = dot(sel_back, dxe_ref[:, cols], 1, 0)
        if more:
            out += join_chunks(old_out, cols).astype(F32)
            dx += join_chunks(old_dx, cols).astype(F32)
        split_chunks(out_refs, cols, out)
        split_chunks(dx_refs, cols, dx)
        return 0

    lax.fori_loop(0, model // wide, combine, 0)


def run_expert(rank, gate, x, dz, w, old, capacity, wide=2048, narrow=1024):
    blocks, rows = rank.shape
    model, feed = x.shape[1], w.shape[1] // 3
    def per_block(r, c): return pl.BlockSpec((r, c), lambda i: (i, 0))
    line = pl.BlockSpec((1, 1, rows), lambda i: (i, 0, 0))
    shape = jax.ShapeDtypeStruct
    slots = blocks * capacity
    more = bool(old)
    form, result = chunk_form(blocks, rows, model)
    xg, dy, hm, dgu, *rest = pl.pallas_call(
        functools.partial(expert_kernel, wide, narrow, more, len(form)),
        grid=(blocks,),
        in_specs=[line, pl.BlockSpec((1, rows, 1), lambda i: (i, 0, 0)), line, per_block(rows, model), per_block(rows, model),
            pl.BlockSpec(w.shape, lambda i: (0, 0), pipeline_mode=pl.Buffered(1))] + form * (2 if more else 0),
        out_specs=[per_block(capacity, model), per_block(capacity, model), per_block(capacity, feed), per_block(capacity, 2 * feed), *form, *form, line],
        out_shape=[shape((slots, model), BF16), shape((slots, model), BF16), shape((slots, feed), BF16), shape((slots, 2 * feed), BF16),
            *result, *result, shape((blocks, 1, rows), F32)],
        scratch_shapes=[pltpu.VMEM((capacity, model), BF16)] * 3 + [pltpu.VMEM((capacity, 128), F32)],
        compiler_params=pltpu.CompilerParams(vmem_limit_bytes=VMEM_LIMIT),
        cost_estimate=BRIEF,
        name="expert",
    )(rank[:, None, :], rank[:, :, None], gate[:, None, :], x, dz, w, *old)
    return xg, dy, hm, dgu, rest[: len(form)], rest[len(form) : -1], rest[-1][:, 0]


def weight_kernel(narrow, xg_ref, dy_ref, dgu_ref, hm_ref, *refs):
    *out_refs, flip_ref = refs
    base = dgu_ref.shape[1] if len(out_refs) == 1 else 0
    for src, other, out_ref, start in ((xg_ref, dgu_ref, out_refs[0], 0), (dy_ref, hm_ref, out_refs[-1], base)):
        flip_ref[...] = src[...].T
        def step(i, _):
            cols = pl.ds(pl.multiple_of(i * narrow, narrow), narrow)
            to = pl.ds(pl.multiple_of(start + i * narrow, narrow), narrow)
            out_ref[:, to] = dot(flip_ref[...], other[:, cols], 1, 0).astype(BF16)
            return 0
        lax.fori_loop(0, other.shape[1] // narrow, step, 0)


def expert_weight_grad(xg, dy, dgu, hm, parts, block=512, narrow=1024):
    slots, model = xg.shape
    feed = hm.shape[1]
    widths = (3 * feed,) if parts == 1 else (2 * feed, feed)
    cut = pl.BlockSpec((slots, block), lambda i: (0, i))
    def whole(c): return pl.BlockSpec((slots, c), lambda i: (0, 0), pipeline_mode=pl.Buffered(1))
    return pl.pallas_call(
        functools.partial(weight_kernel, narrow),
        grid=(model // block,),
        in_specs=[cut, cut, whole(2 * feed), whole(feed)],
        out_specs=[pl.BlockSpec((block, c), lambda i: (i, 0)) for c in widths],
        out_shape=[jax.ShapeDtypeStruct((model, c), BF16) for c in widths],
        scratch_shapes=[pltpu.VMEM((block, slots), BF16)],
        compiler_params=pltpu.CompilerParams(vmem_limit_bytes=VMEM_LIMIT),
        cost_estimate=BRIEF,
        name="expert_weight_grad",
    )(xg, dy, dgu, hm)

def adam_kernel(rate, w_ref, g_ref, m_ref, v_ref, *refs):
    m_out, v_out, w_out = refs[-3:]
    new = adam_step(w_ref[0], g_ref[...], m_ref[0], v_ref[0], rate)
    m_out[0], v_out[0], w_out[0] = new

def adam_part(e, base, weight, grad, first, second, old, rate, block=128, wide=1024):
    rows, cols = grad.shape
    block = min(block, rows)
    one = pl.BlockSpec((1, block, wide), lambda i, j: (e, i, base // wide + j))
    out = jax.ShapeDtypeStruct(weight.shape, F32)
    old = tuple(old or ())
    return pl.pallas_call(
        functools.partial(adam_kernel, rate),
        grid=(rows // block, cols // wide),
        in_specs=[one, pl.BlockSpec((block, wide), lambda i, j: (i, j)), one, one]
        + [pl.BlockSpec(memory_space=pl.ANY)] * len(old),
        out_specs=[one] * 3,
        out_shape=[out] * 3,
        input_output_aliases={4 + i: i for i in range(len(old))},
        compiler_params=pltpu.CompilerParams(vmem_limit_bytes=VMEM_LIMIT),
        cost_estimate=BRIEF,
        name="adam_part",
    )(weight, grad, first, second, *old)


def norm_back(dn, value, gain):
    scale = lax.rsqrt(jnp.mean(value * value, axis=-1, keepdims=True) + NORM_EPS)
    hat = value * scale
    inner = dn * gain
    back = scale * (inner - hat * jnp.mean(inner * hat, axis=-1, keepdims=True))
    return back, jnp.sum(dn * hat, axis=0)


def after(value, *others):
    return lax.optimization_barrier((value, *others))[0]


def body(
    tokens,
    cotangent,
    doc_lengths,
    routes,
    attn_weight,
    router_weight,
    gain_values,
    expert_weight,
    attn_first,
    attn_second,
    router_first,
    router_second,
    gain_first,
    gain_second,
    expert_first,
    expert_second,
):
    fsdp_count, seq_count = lax.axis_size("fsdp"), lax.axis_size("seq")
    everywhere = ("seq", "fsdp")
    here, plane = lax.axis_index("fsdp"), lax.axis_index("seq")
    around = here ^ jnp.arange(fsdp_count, dtype=jnp.int32)
    planes = plane ^ jnp.arange(seq_count, dtype=jnp.int32)
    rows, model = tokens.shape[1:]
    length = rows * seq_count
    experts = EXP_DEV * fsdp_count
    capacity = (rows * TOP // experts * 4 // 3 + 7) // 8 * 8
    width = model // fsdp_count
    shard = attn_weight.shape[0]
    members, chunk = fsdp_count // seq_count, rows // fsdp_count
    blocks = fsdp_count

    def blocked(parts):
        stacked = jnp.stack([part.reshape(blocks, chunk, -1) for part in parts], axis=1)
        return stacked.reshape(blocks * rows, -1)

    def pieces(value):
        cut = value.reshape(blocks, fsdp_count, chunk, -1)
        return [cut[:, k].reshape(rows, -1) for k in range(fsdp_count)]

    with jax.named_scope("gather_wo"):
        out_part = gather_direct(attn_weight[:, 3 * model :], "seq", seq_count)
    with jax.named_scope("remap_x"):
        x_parts = reorder(tokens[0].reshape(fsdp_count, chunk, model), around)
        x_parts = reorder(jnp.stack(exchange(list(x_parts), "fsdp", fsdp_count)), around)
        x_low = to_plane_seq(x_parts, seq_count, fsdp_count)
    with jax.named_scope("gather_wqkv"):
        first_part = attn_weight[:, : 3 * model].reshape(shard, 3, fsdp_count, width).transpose(2, 0, 1, 3)
        first_part = reorder(first_part.reshape(fsdp_count, shard, 3 * width), around)
        first_part = reorder(jnp.stack(exchange(list(first_part), "fsdp", fsdp_count)), around)
        in_proj = lax.all_gather(first_part.reshape(fsdp_count * shard, 3 * width), "seq", axis=0, tiled=True)
    with jax.named_scope("gather_small"):
        flat = [router_weight.reshape(-1), gain_values, routes.reshape(-1), doc_lengths.reshape(-1)]
        sizes = [v.shape[0] for v in flat]
        starts = [sum(sizes[:i]) for i in range(len(sizes))]
        flat = after(jnp.concatenate([v.astype(F32) for v in flat]), x_low)
        flat = jnp.pad(flat, (0, -flat.shape[0] % 1024)).reshape(-1, 128)
        lines = flat.shape[0]
        small_all = lax.all_gather(flat, "seq", axis=0, tiled=True)
        small_all = lax.all_gather(small_all, "fsdp", axis=0, tiled=True)
        every = small_all.reshape(fsdp_count, seq_count, lines * 128)
        per_device = every.transpose(1, 0, 2).reshape(seq_count * fsdp_count, lines * 128)
        full_router = per_device[:, : sizes[0]].reshape(model, experts).astype(BF16)
        gains = per_device[:, starts[1] : starts[2]].reshape(-1)
        attn_gain, ffn_gain = gains[:model], gains[model : 2 * model]
        gain_q = gains[2 * model : 2 * model + HDIM][None]
        gain_k = gains[2 * model + HDIM : 2 * model + 2 * HDIM][None]
        meta = lax.dynamic_slice_in_dim(every, plane * members, members, 0)[:, :, starts[2] : starts[3] + 3]
        meta = meta.astype(jnp.int32)
    docs = meta[:, 0, rows * TOP : rows * TOP + 3]
    routes_all = meta[:, :, : rows * TOP].reshape(blocks, fsdp_count, chunk, TOP)
    routes_all = reorder(routes_all, around, 1).reshape(blocks, rows, TOP)
    positions = (
        jnp.arange(seq_count, dtype=jnp.int32)[:, None, None] * rows
        + around[None, :, None] * chunk
        + jnp.arange(chunk, dtype=jnp.int32)[None, None, :]
    ).reshape(1, length)
    doc_index = (positions >= docs[:, :1]).astype(jnp.int32) + (
        positions >= docs[:, :1] + docs[:, 1:2]
    ).astype(jnp.int32)
    row_doc, col_doc = doc_index[:, :, None], doc_index[:, None, :]
    frequency = ROPE_BASE ** (-jnp.arange(HDIM // 2, dtype=F32) / (HDIM // 2))
    angles = positions[0].astype(F32)[:, None] * frequency[None, :]
    cosine, sine = jnp.cos(angles), jnp.sin(angles)
    cosine = jnp.concatenate([cosine, cosine], axis=1)
    sine = jnp.concatenate([-sine, sine], axis=1)

    with jax.named_scope("gather_experts"):
        expert_later = after(expert_weight, first_part)
        expert_full = [lax.all_gather(expert_later[e], "seq", axis=0, tiled=True) for e in range(EXP_DEV)]
    with jax.named_scope("gather_wo"):
        out_part = jnp.stack(plane_gather(fsdp_count, out_part.reshape(seq_count * shard, model)))
        out_part = out_part.reshape(fsdp_count * seq_count, shard, model)
        place = jnp.arange(seq_count * fsdp_count, dtype=jnp.int32)
        place = (here ^ (place % fsdp_count)) * seq_count + (plane ^ (place // fsdp_count))
        out_proj = reorder(out_part, place).reshape(model, model)
    with jax.named_scope("gather_x"):
        x_all = blocked(plane_gather(fsdp_count, x_low))
    with jax.named_scope("remap_dz"):
        dz_low = to_plane_seq(to_plane_fsdp(after(cotangent[0], x_all), fsdp_count), seq_count, fsdp_count)

    own = here * EXP_DEV + jnp.arange(EXP_DEV, dtype=jnp.int32)
    named = jnp.any(routes_all[:, None, :, :] == own[None, :, None, None], axis=3)
    before = jnp.cumsum(named.astype(jnp.int32), axis=2) - named.astype(jnp.int32)
    rank = jnp.where(named, before, -1)
    chosen = jnp.any(
        routes_all[:, :, :, None] == jnp.arange(experts, dtype=jnp.int32)[None, None, None, :], axis=2
    )

    cosine_all, sine_all = jnp.tile(cosine, (members, 1)), jnp.tile(sine, (members, 1))
    a_all, q_low, k_low, v_low, q_pre, k_pre = project(
        x_all, attn_gain[None], in_proj, cosine_all, sine_all, gain_q, gain_k, rows
    )
    with jax.named_scope("gather_dz"):
        dz_all = blocked(plane_gather(fsdp_count, dz_low))
    seq_shape = (members, length, width)
    q_seq, k_seq, v_seq = (t.reshape(seq_shape) for t in (q_low, k_low, v_low))
    o_all = attend(q_seq, k_seq, v_seq, row_doc, col_doc)
    with jax.named_scope("o_exchange"):
        o_own = reorder(o_all.reshape(blocks, fsdp_count, chunk, width), around, 1)
        o_own = o_own.transpose(1, 0, 2, 3).reshape(fsdp_count, rows, width)
        o_own = lax.all_to_all(o_own, "fsdp", split_axis=0, concat_axis=0, tiled=True)
        o_own = o_own.transpose(1, 0, 2).reshape(rows, model)
    inputs = x_low.astype(F32)
    middle = inputs + dot(o_own, out_proj, 1, 0)
    middle_scale = lax.rsqrt(jnp.mean(middle * middle, axis=-1, keepdims=True) + NORM_EPS)
    normed = (middle * middle_scale * ffn_gain).astype(BF16)

    with jax.named_scope("gather_xn"):
        xn_all = blocked(plane_gather(fsdp_count, normed))
    with jax.named_scope("gates"):
        logits = dot(xn_all, full_router, 1, 0).reshape(blocks, rows, experts)
        top = jnp.max(jnp.where(chosen, logits, -jnp.inf), axis=2, keepdims=True)
        raised = jnp.where(chosen, jnp.exp(logits - top), 0.0)
        gates = raised / jnp.sum(raised, axis=2, keepdims=True)
        gates_mine = lax.dynamic_slice_in_dim(gates, here * EXP_DEV, EXP_DEV, axis=2)
    sums, gate_back, expert_share, held = (), [], [], None
    for e in range(EXP_DEV):
        with jax.named_scope(f"expert{e}"):
            w = expert_full[e] if held is None else after(expert_full[e], *held)
            xg, dy, hm, dgu, mixed, dxn, dgate = run_expert(
                rank[:, e], gates_mine[:, :, e], xn_all, dz_all, w, sums, capacity
            )
            sums = (*mixed, *dxn)
            gate_back.append(dgate)
            if e == EXP_DEV - 1:
                gate_parts = exchange(pieces(jnp.stack(gate_back, axis=2)), "fsdp", fsdp_count)
                dxn = Scatter(fsdp_count, *by_owner(dxn, blocks), hold=gate_parts)
                xg = after(xg, *dxn.sends)
            held = expert_weight_grad(xg, dy, dgu, hm, 1 if e < EXP_DEV - 1 else 2)
            if e < EXP_DEV - 1:
                expert_share.append(lax.psum_scatter(held[0], "seq", scatter_dimension=0, tiled=True))
    last_up = lax.psum_scatter(held[0], "seq", scatter_dimension=0, tiled=True)

    with jax.named_scope("router_back"):
        gate_grad = reorder(jnp.stack(gate_parts, axis=1), around, 1).reshape(rows, experts)
        gates_own, chosen_own = pieces(gates)[0], pieces(chosen)[0]
        gate_grad = jnp.where(chosen_own, gate_grad, 0.0)
        dlog = (gates_own * (gate_grad - jnp.sum(gates_own * gate_grad, axis=1, keepdims=True))).astype(BF16)
    with jax.named_scope("scatter_dxn"):
        dxn_own = dxn.second(*held).third()
    dxn_own = dxn_own + dot(dlog, full_router, 1, 1)
    middle_back, ffn_gain_grad = norm_back(dxn_own, middle, ffn_gain)
    middle_grad = dz_low.astype(F32) + middle_back
    db = middle_grad.astype(BF16)

    with jax.named_scope("do_exchange"):
        do_own = dot(db, out_proj, 1, 1).astype(BF16).reshape(rows, fsdp_count, width).transpose(1, 0, 2)
        do_own = lax.all_to_all(do_own, "fsdp", split_axis=0, concat_axis=0, tiled=True)
        do_all = reorder(do_own, around).reshape(fsdp_count, blocks, chunk, width).transpose(1, 0, 2, 3)
        do_all = do_all.reshape(seq_shape)
    with jax.named_scope("scatter_out"):
        near, far = by_owner(mixed, blocks)
        mixed = Scatter(fsdp_count, near, after(far, db), hold=(do_all,))
    do_all = after(do_all, expert_share[0], *mixed.sends)
    dq, dk, dv = (
        t.reshape(-1, width) for t in attend_back(q_seq, k_seq, v_seq, do_all, row_doc, col_doc)
    )
    with jax.named_scope("scatter_out"):
        mixed = mixed.second(dq)
    d_proj, gain_qk, *da_part = project_back(
        after(dq, *mixed.lasts), dk, dv, q_pre, k_pre, cosine_all, sine_all, gain_q, gain_k, in_proj, rows
    )
    with jax.named_scope("scatter_out"):
        layer_low = (middle + mixed.third(d_proj)).astype(BF16)
    with jax.named_scope("scatter_da"):
        near, far = by_owner(da_part, blocks)
        da = Scatter(fsdp_count, near, after(far, layer_low))
    with jax.named_scope("remap_out"):
        layer_out = from_plane_seq(layer_low, seq_count, fsdp_count)
    with jax.named_scope("weight_grads"):
        in_grad = dot(after(a_all, *da.sends), d_proj, 0, 0).astype(BF16)
        in_share = lax.psum_scatter(in_grad, "seq", scatter_dimension=0, tiled=True)
        moments = (expert_first, expert_second)
        expert_new = None
        for e in range(EXP_DEV - 1):
            share = after(expert_share[e], *da.sends)
            expert_new = adam_part(e, 0, expert_weight, share, *moments, expert_new, RATE_EXPERT)
    with jax.named_scope("scatter_da"):
        da = da.second(in_grad, expert_new[0])
    last_down = lax.psum_scatter(after(held[1], *da.lasts), "seq", scatter_dimension=0, tiled=True)
    with jax.named_scope("weight_grads"):
        out_grad = dot(after(o_own, *da.lasts), db, 0, 0).astype(BF16)
        out_grad = out_grad.reshape(seq_count, fsdp_count, shard, model)
        pairs = reorder(around, jnp.arange(fsdp_count).reshape(-1, 2).T.reshape(-1))
        out_grad = reorder(out_grad, pairs, 1).transpose(1, 0, 2, 3)
        out_grad = out_grad.reshape(2, fsdp_count // 2, seq_count * shard, model)
    with jax.named_scope("scatter_da"):
        da_own = da.third(out_grad, layer_out)
    input_back, attn_gain_grad = norm_back(da_own, inputs, attn_gain)
    input_low = (middle_grad + input_back).astype(BF16)
    with jax.named_scope("remap_grad"):
        input_grad = from_plane_seq(input_low, seq_count, fsdp_count)
    with jax.named_scope("small_sum"):
        router_grad = dot(normed, dlog, 0, 0)
        small = jnp.concatenate(
            [router_grad.reshape(-1), attn_gain_grad, ffn_gain_grad, gain_qk[0], gain_qk[1]]
        )
        small = plane_sum(small, fsdp_count)
        own_router, own_gain = shard * experts, gain_values.shape[0]

        def own_part(p):
            device = p * fsdp_count + here
            return jnp.concatenate(
                [
                    lax.dynamic_slice_in_dim(small, device * own_router, own_router),
                    lax.dynamic_slice_in_dim(small, model * experts + device * own_gain, own_gain),
                ]
            )

        small_parts = [own_part(planes[m]) for m in range(seq_count)]
    with jax.named_scope("scatter_wo"):
        out_grad = Scatter(fsdp_count, out_grad[0], after(out_grad[1], input_low), hold=small_parts)
    last = EXP_DEV - 1
    expert_new = adam_part(
        last, 0, expert_weight, after(last_up, *out_grad.sends), *moments, expert_new, RATE_EXPERT
    )
    with jax.named_scope("scatter_wo"):
        out_grad = out_grad.second(expert_new[0])
        out_share = out_grad.third().astype(BF16)
    with jax.named_scope("scatter_wo"):
        out_sent = reorder(out_share.reshape(seq_count, shard, model), planes)
        out_parts = exchange(list(out_sent), "seq", seq_count)
    with jax.named_scope("scatter_wqkv"):
        in_share = after(in_share, out_sent)
        in_share = sent = reorder(in_share.reshape(fsdp_count, shard, 3 * width), around)
        in_share = reorder(jnp.stack(exchange(list(in_share), "fsdp", fsdp_count)), around)
        in_share = in_share.reshape(fsdp_count, shard, 3, width).transpose(1, 2, 0, 3).reshape(shard, 3 * model)
    with jax.named_scope("remap"):
        both = jnp.concatenate([input_grad, layer_out], axis=1)
        both = from_plane_fsdp(after(both, sent), fsdp_count)
        input_grad, layer_out = both[:, :model].astype(F32), both[:, model:]
    small_own = sum(exchange(list(lax.optimization_barrier((*small_parts, in_share))[:-1]), "seq", seq_count))
    router_share, gain_share = small_own[:own_router].reshape(shard, experts), small_own[own_router:]

    attn_states = [v[None] for v in (attn_weight, attn_first, attn_second)]
    attn_new = adam_part(0, 0, attn_states[0], in_share, *attn_states[1:], None, RATE_ATTN, wide=2048)
    router_new = adam_step(router_weight, router_share, router_first, router_second, RATE_ROUTER)
    last_down, input_grad, layer_out, _ = lax.optimization_barrier(
        (last_down, input_grad, layer_out, attn_new[0])
    )
    expert_new = adam_part(
        last,
        2 * FFE,
        expert_weight,
        last_down,
        *moments,
        expert_new,
        RATE_EXPERT,
        block=256,
    )
    out_parts = lax.optimization_barrier((*out_parts, expert_new[0]))[:-1]
    out_share = sum(p.astype(F32) for p in out_parts)
    attn_new = adam_part(
        0, 3 * model, attn_states[0], out_share, *attn_states[1:], attn_new, RATE_ATTN
    )
    attn_new = [v[0] for v in attn_new]
    gain_new = adam_step(gain_values, gain_share, gain_first, gain_second, RATE_GAIN)
    return (layer_out[None], input_grad[None], *attn_new, *router_new, *gain_new, *expert_new)


def solution(mesh):
    tokens = P("fsdp", "seq", None)
    matrix, vector = P(("seq", "fsdp"), None), P(("seq", "fsdp"))
    return jax.shard_map(
        body,
        mesh=mesh,
        in_specs=(
            tokens,
            tokens,
            P("fsdp", None),
            tokens,
            matrix,
            matrix,
            vector,
            tokens,
            matrix,
            matrix,
            matrix,
            matrix,
            vector,
            vector,
            tokens,
            tokens,
        ),
        out_specs=(
            tokens,
            tokens,
            matrix,
            matrix,
            matrix,
            matrix,
            matrix,
            matrix,
            vector,
            vector,
            vector,
            tokens,
            tokens,
            tokens,
        ),
        check_vma=False,
    )
```
